128 devices in a mesh: grp: 8 (over x, core), head: 16 (over z, y).
Axes of the slice: x: 4, y: 4, z: 4, core: 2. Of those that a mesh axis runs over, the one named last changes fastest.
Arguments:
- request_owner: int32 [256], P('grp'), parts along dimension 0, may hold values from 0 to 15, as said below
- page_list: int32 [256, 8], P('grp'), parts along dimension 0, may hold values from 0 to 255, as said below
- context_len: int32 [256], P('grp'), parts along dimension 0, may hold values from 1 to 1024, as said below
- lin_state: float32 [256, 64, 128, 128], P('grp', 'head'), parts along dimension 0, may hold values from -6 to 6
- decay_rate: float32 [64], replicated, may hold values from 0.02 to 3
- lin_query: bfloat16 [256, 2, 8192], P(('grp', 'head')), parts along dimension 0, may hold values from -0.5 to 0.5
- lin_keyval: bfloat16 [256, 2, 2, 8192], P(('grp', 'head')), parts along dimension 0, may hold values from -5 to 5
- soft_query: bfloat16 [256, 2, 8192], P(('grp', 'head')), parts along dimension 0, may hold values from -10 to 10
- new_keyval: bfloat16 [256, 2, 2, 1024], P(('grp', 'head')), parts along dimension 0, may hold values from -4 to 4
- page_pool: bfloat16 [2048, 2, 128, 1024], P(('grp', 'head')), parts along dimension 0, may hold values from -4 to 4
Outputs:
- lin_out: float32 [256, 2, 8192], P(('grp', 'head')), parts along dimension 0
- soft_out: float32 [256, 2, 8192], P(('grp', 'head')), parts along dimension 0
The draws below stay inside these ranges and needn't reach their ends.
There are 8 independent parts, one for each index of `grp`. The reference program is written for one: setup_inputs(seed, part) draws one part's arguments, and reference() takes and returns one part's arrays. A program takes and returns all parts, laid end to end along the dimension named above; an argument that names none is the same for every part. Nothing has to cross between parts.
Inputs may be any that keep to these rules, and one draw needn't show every extreme that they name: `request_owner`: each owner 0 .. 15 names exactly 2 requests. `page_list`: all entries of the table are distinct, so every pool page is listed once. Pages 16 * d .. 16 * d + 15 lie on device d of head; among them at most 2 are listed by the requests of one owner, exactly 2 for some device and owner. Entries j with j * 128 >= context_len of the request are padding. `context_len`: some request has exactly 1024 cached tokens.
All inputs are finite; a program needn't handle non-finite values.
Results may differ from the reference program's by a relative error of at most 0.0012.
Values may be sent and summed in bfloat16 or wider, within the bound.
A program may use at most 128 MiB of HBM per device.

```python
import math
import jax
import jax.numpy as jnp
from jax import lax

HEADS = 64
HDIM = 128
KVH = 8
PAGE = 128
STEPS = 2
RPD = 2
MAXP = 8
REQS = 32
OWNER_PAGES = 16
POOL_PAGES = 256
CTX_MAX = 1024
N_HEAD = 16


def layout_tables(key):
    total = RPD * N_HEAD
    key_req, key_dev, key_order, key_surplus, key_mixing = jax.random.split(key, 5)
    shuffled = jax.random.permutation(key_req, total).astype(jnp.int32)
    request_owner = (shuffled // RPD).astype(jnp.int32)
    index = jnp.arange(total, dtype=jnp.int32)
    same = request_owner[:, None] == request_owner[None, :]
    earlier = index[None, :] < index[:, None]
    slots = jnp.sum(jnp.where(same & earlier, 1, 0), axis=1).astype(jnp.int32)
    repeat = OWNER_PAGES // N_HEAD
    surplus = jax.random.permutation(key_surplus, N_HEAD).astype(jnp.int32)
    mixing = jax.random.permutation(key_mixing, N_HEAD).astype(jnp.int32)
    swapped = mixing.at[0].set(mixing[1]).at[1].set(mixing[0])
    mixing = jnp.where(mixing[0] == 0, swapped, mixing).astype(jnp.int32)
    deficit = jnp.take(surplus, mixing, axis=0).astype(jnp.int32)
    baseline = (jnp.arange(OWNER_PAGES, dtype=jnp.int32) // repeat)[None, :]
    holder_sorted = jnp.where(baseline == deficit[:, None], surplus[:, None], baseline).astype(jnp.int32)
    owner_keys = jax.random.split(key_dev, N_HEAD)
    shuffle_order = jax.vmap(lambda single: jax.random.permutation(single, OWNER_PAGES))(owner_keys).astype(jnp.int32)
    holder = jnp.take_along_axis(holder_sorted, shuffle_order, axis=1).astype(jnp.int32)
    count = N_HEAD * OWNER_PAGES
    tiebreak = jax.random.permutation(key_order, count).astype(jnp.int32)
    sortkey = holder.reshape(-1) * count + tiebreak
    ordering = jnp.argsort(sortkey).astype(jnp.int32)
    page_of_slot = jnp.zeros((count,), jnp.int32).at[ordering].set(jnp.arange(count, dtype=jnp.int32))
    start = request_owner * OWNER_PAGES + slots * MAXP
    page_list = jnp.take(page_of_slot, start[:, None] + jnp.arange(MAXP, dtype=jnp.int32)[None, :], axis=0)
    return (request_owner, page_list.astype(jnp.int32))


def draw_request_owner(key, part):
    owners, listed = layout_tables(key)
    return owners


def draw_page_list(key, part):
    owners, listed = layout_tables(key)
    return listed


def draw_context_len(key, part):
    key = jax.random.fold_in(key, 3)
    total = RPD * N_HEAD
    key_level, key_drop, key_pick = jax.random.split(key, 3)
    level = jax.random.randint(key_level, (total,), 0, 4)
    upper = jnp.where(level == 3, CTX_MAX // 2, CTX_MAX).astype(jnp.int32)
    drop = jax.random.randint(key_drop, (total,), 0, upper // 4 + 1)
    lengths = upper - drop
    chosen = jax.random.randint(key_pick, (), 0, total)
    return jnp.where(jnp.arange(total) == chosen, CTX_MAX, lengths).astype(jnp.int32)


def draw_new_keyval(key, part):
    key = jax.random.fold_in(key, 5)
    total = RPD * N_HEAD
    shape = (total, STEPS, 2, KVH * HDIM)
    values = jnp.clip(jax.random.normal(key, shape, jnp.float32), -4.0, 4.0)
    return values.astype(jnp.bfloat16)


def draw_soft_query(key, part):
    key = jax.random.fold_in(key, 7)
    total = RPD * N_HEAD
    shape = (total, STEPS, HEADS * HDIM)
    values = jnp.clip(2.0 * jax.random.normal(key, shape, jnp.float32), -8.0, 8.0)
    return values.astype(jnp.bfloat16)


def draw_page_pool(key, part):
    key = jax.random.fold_in(key, 11)
    shape = (POOL_PAGES, 2, PAGE, KVH * HDIM)
    pool = jnp.clip(jax.random.normal(key, shape, jnp.float32), -4.0, 4.0)
    return pool.astype(jnp.bfloat16)


def steps_of(key, extent, pieces, low, high):
    loudness, own = 1.0, jax.random.fold_in(key, 6)
    for axis_at, shards_of in pieces:
        steps = jnp.exp(jax.random.uniform(jax.random.fold_in(own, axis_at), (shards_of,), jnp.float32, low / len(pieces), high / len(pieces)))
        loudness = loudness * jnp.repeat(steps, extent[axis_at] // shards_of).reshape([-1 if axis == axis_at else 1 for axis in range(len(extent))])
    return loudness


def centred(rng, extent, scale, reach, shards=(), kind=jnp.bfloat16):
    drawn = jax.random.normal(rng, extent, jnp.float32) * scale
    if len(shards) > 0:
        drawn = steps_of(rng, extent, shards, -0.22, 0.18) * drawn
    return jnp.clip(drawn, min=-reach, max=reach).astype(kind)


def setup_inputs(seed: int = 0, part: int = 0) -> dict:
    seeds = jax.random.split(jax.random.key(seed), 11)
    part_keys = jax.random.split(jax.random.fold_in(seeds[10], part), 11)
    return {
        "request_owner": draw_request_owner(jax.random.fold_in(jax.random.fold_in(seeds[10], part), 71), part),
        "page_list": draw_page_list(jax.random.fold_in(jax.random.fold_in(seeds[10], part), 71), part),
        "context_len": draw_context_len(jax.random.fold_in(jax.random.fold_in(seeds[10], part), 71), part),
        "lin_state": centred(part_keys[3], (REQS, HEADS, HDIM, HDIM), 1.0, 6.0, ((1, 16),), jnp.float32),
        "decay_rate": jnp.clip(jnp.exp(jax.random.uniform(seeds[4], (HEADS,), jnp.float32, math.log(0.02), math.log(3.0))), 0.02, 3.0),
        "lin_query": centred(part_keys[5], (REQS, STEPS, HEADS * HDIM), HDIM ** -0.5, 0.5, ((0, 16),)),
        "lin_keyval": centred(part_keys[6], (REQS, STEPS, 2, HEADS * HDIM), 1.0, 5.0, ((0, 16),)),
        "soft_query": draw_soft_query(jax.random.fold_in(jax.random.fold_in(seeds[10], part), 71), part),
        "new_keyval": draw_new_keyval(jax.random.fold_in(jax.random.fold_in(seeds[10], part), 71), part),
        "page_pool": draw_page_pool(jax.random.fold_in(jax.random.fold_in(seeds[10], part), 71), part),
    }


def row_tables(request_owner, per_owner):
    total = request_owner.shape[0]
    index = jnp.arange(total, dtype=jnp.int32)
    same = request_owner[:, None] == request_owner[None, :]
    earlier = index[None, :] < index[:, None]
    slots = lax.optimization_barrier(jnp.sum(jnp.where(same & earlier, 1, 0), axis=1)).astype(jnp.int32)
    row_of = (request_owner * per_owner + slots).astype(jnp.int32)
    match = row_of[None, :] == index[:, None]
    request_of = lax.optimization_barrier(jnp.sum(jnp.where(match, index[None, :], 0), axis=1)).astype(jnp.int32)
    return (row_of, request_of)

def lightning(state, query, keyval, rates):
    batch, heads_n, width = (state.shape[0], state.shape[1], state.shape[2])
    factor = jnp.exp(-rates)[None, :, None, None]
    outputs = []
    for step in range(keyval.shape[1]):
        keys = keyval[:, step, 0].astype(jnp.float32).reshape(batch, heads_n, width)
        values = keyval[:, step, 1].astype(jnp.float32).reshape(batch, heads_n, width)
        state = factor * state + keys[:, :, :, None] * values[:, :, None, :]
        query_now = query[:, step].astype(jnp.float32).reshape(batch, heads_n, width)
        mixed = jnp.einsum('bhd,bhde->bhe', query_now, state, precision=lax.Precision.HIGHEST)
        spread = jnp.sqrt(lax.optimization_barrier(jnp.mean(mixed * mixed, axis=-1, keepdims=True)) + 1e-05)
        outputs.append((mixed / spread).reshape(batch, heads_n * width))
    return jnp.stack(outputs, axis=1)

def page_partial(query, keys, values, live):
    scores = jnp.einsum('tkgd,nkd->tkgn', query.astype(jnp.float32), keys.astype(jnp.float32), precision=lax.Precision.HIGHEST) * (1.0 / math.sqrt(query.shape[-1]))
    mask = live[:, None, None, :]
    top = lax.optimization_barrier(jnp.max(jnp.where(mask, scores, -1e+30), axis=-1))
    weights = jnp.where(mask, jnp.exp(scores - top[..., None]), 0.0)
    total = lax.optimization_barrier(jnp.sum(weights, axis=-1))
    rounded = lax.optimization_barrier(weights.astype(jnp.bfloat16))
    acc = jnp.einsum('tkgn,nkd->tkgd', rounded.astype(jnp.float32), values.astype(jnp.float32), precision=lax.Precision.HIGHEST)
    return (top, total, acc)

def merge_blocks(tops, totals, accs, axis):
    peak = lax.optimization_barrier(jnp.max(tops, axis=axis, keepdims=True))
    factor = jnp.exp(tops - peak)
    denom = lax.optimization_barrier(jnp.sum(factor * totals, axis=axis))
    numer = lax.optimization_barrier(jnp.sum(factor[..., None] * accs, axis=axis))
    return numer / denom[..., None]

def attend(query, fresh, pages, length):
    steps = query.shape[0]
    kvh = fresh.shape[-1] // HDIM
    group = HEADS // kvh
    size = pages.shape[2]
    grouped = query.reshape(steps, kvh, group, HDIM)

    def one_page(page, count):
        live = jnp.broadcast_to(jnp.arange(size, dtype=jnp.int32)[None, :] < count, (steps, size))
        return page_partial(grouped, page[0].reshape(size, kvh, HDIM), page[1].reshape(size, kvh, HDIM), live)
    counts = jnp.clip(length - jnp.arange(pages.shape[0], dtype=jnp.int32) * size, 0, size).astype(jnp.int32)
    tops, totals, accs = jax.vmap(one_page)(pages, counts)
    live_new = jnp.arange(steps)[None, :] <= jnp.arange(steps)[:, None]
    top_new, total_new, acc_new = page_partial(grouped, fresh[:, 0].reshape(steps, kvh, HDIM), fresh[:, 1].reshape(steps, kvh, HDIM), live_new)
    result = merge_blocks(jnp.concatenate([tops, top_new[None]], axis=0), jnp.concatenate([totals, total_new[None]], axis=0), jnp.concatenate([accs, acc_new[None]], axis=0), 0)
    return result.reshape(steps, HEADS * HDIM)

def reference(request_owner, page_list, context_len, lin_state, decay_rate, lin_query, lin_keyval, soft_query, new_keyval, page_pool):
    row_of, request_of = row_tables(request_owner, RPD)
    query_req = jnp.take(lin_query, row_of, axis=0)
    keyval_req = jnp.take(lin_keyval, row_of, axis=0)

    def lin_one(items):
        return lightning(items[0][None], items[1][None], items[2][None], decay_rate)[0]
    by_request = lax.map(lin_one, (lin_state, query_req, keyval_req))
    lin_out = jnp.take(by_request, request_of, axis=0)

    def soft_one(items):
        query, fresh, request = items
        pages = jnp.take(page_pool, page_list[request], axis=0)
        return attend(query, fresh, pages, context_len[request])
    soft_out = lax.map(soft_one, (soft_query, new_keyval, request_of))
    return (lin_out, soft_out)
```

```python
import functools
import math

import jax
import jax.numpy as jnp
from jax import lax
from jax.experimental import pallas as pl
from jax.experimental.pallas import tpu as pltpu
from jax.sharding import PartitionSpec as P

MESH = pl.DeviceIdType.MESH
N = 16
WIDTH = 128
KVH = 8
CODES = 32000.0
LOW = -1e30
SCALE = 1.0 / math.sqrt(128.0)


def tables(request_owner, page_list, context_len, me):
    total = request_owner.shape[0]
    index = jnp.arange(total, dtype=jnp.int32)
    same = request_owner[:, None] == request_owner[None, :]
    earlier = index[None, :] < index[:, None]
    slots = jnp.sum(jnp.where(same & earlier, 1, 0), axis=1).astype(jnp.int32)
    row_of = request_owner * 2 + slots
    request_of = jnp.sum(jnp.where(row_of[None, :] == index[:, None], index[None, :], 0), axis=1)
    span = page_list.shape[1]
    here = page_list // 16 == me
    entry = row_of[:, None] * span + jnp.arange(span, dtype=jnp.int32)[None, :]
    count = jnp.clip(context_len[:, None] - jnp.arange(span, dtype=jnp.int32)[None, :] * WIDTH, 0, WIDTH)
    here, entry, count = here.reshape(-1), entry.reshape(-1), count.reshape(-1)
    local = (page_list % 16).reshape(-1)
    before = here[None, :] & (entry[None, :] // 16 == entry[:, None] // 16) & (entry[None, :] < entry[:, None])
    slot = jnp.where(here, entry // 16 * 2 + jnp.sum(jnp.where(before, 1, 0), axis=1), -1)
    packed = local + entry // 8 % 2 * 16 + count * 32
    slot_codes = jnp.sum(
        jnp.where(slot[None, :] == jnp.arange(2 * N, dtype=jnp.int32)[:, None], packed[None, :], 0), axis=1
    )
    return jnp.concatenate([request_of, slot_codes]).astype(jnp.int32)


def kernel(
    tab, rate, lq, lkv, sq, nkv, state_hbm, pool_hbm, lin_ref, soft_ref,
    state, pool, q_all, lq_in, lkv_in, lin_send, lin_in, res_send, res_in, meta_send, meta_in, run_acc, run_meta,
    local_sem, send_sem, recv_sem,
):
    me = lax.axis_index("head")
    mz, my = me // 4, me % 4

    def ahead(i):
        return (mz + i // 4) % 4 * 4 + (my + i % 4) % 4

    def behind(i):
        return (mz + 4 - i // 4) % 4 * 4 + (my + 4 - i % 4) % 4

    def remote(src, dst, kind, i, to):
        return pltpu.make_async_remote_copy(
            src_ref=src, dst_ref=dst, send_sem=send_sem.at[kind, i], recv_sem=recv_sem.at[kind, i],
            device_id={"head": to}, device_id_type=MESH,
        )

    def lin_part(i):
        to = ahead(i)
        lanes = pl.ds(pl.multiple_of(to * 512, 512), 512)
        return (
            remote(lq.at[:, :, lanes], lq_in.at[i], 0, i, to),
            remote(lkv.at[:, :, :, lanes], lkv_in.at[i], 1, i, to),
        )

    def query(i):
        return remote(q_all.at[0], q_all.at[i], 2, i, ahead(i))

    def lin_back(i):
        return remote(lin_send.at[i], lin_in.at[me], 3, i, behind(i))

    def result(i):
        return remote(res_send.at[i], res_in.at[i], 4, i, behind(i))

    def meta(i):
        return remote(meta_send.at[i], meta_in.at[i], 5, i, behind(i))

    barrier = pltpu.get_barrier_semaphore()

    def greet(i, carry):
        pl.semaphore_signal(barrier, inc=1, device_id={"head": ahead(i)}, device_id_type=MESH)
        return carry

    lax.fori_loop(1, N, greet, 0)
    fetch_state = pltpu.make_async_copy(state_hbm, state, local_sem.at[0])
    fetch_pool = pltpu.make_async_copy(pool_hbm, pool, local_sem.at[1])
    fetch_state.start()
    fetch_pool.start()
    own_lanes = pl.ds(pl.multiple_of(me * 512, 512), 512)
    own_q = pltpu.make_async_copy(lq.at[:, :, own_lanes], lq_in.at[0], local_sem.at[2])
    own_kv = pltpu.make_async_copy(lkv.at[:, :, :, own_lanes], lkv_in.at[0], local_sem.at[3])
    own_q.start()
    own_kv.start()
    for r in range(2):
        wide = sq[r].astype(jnp.float32)
        q_all[0, r] = jnp.concatenate(
            [wide[:, h * WIDTH:(h + 1) * WIDTH] for h in range(64)], axis=0
        ).astype(jnp.bfloat16)
    pl.semaphore_wait(barrier, N - 1)

    def send_lin(i, carry):
        a, b = lin_part(i)
        a.start()
        b.start()
        return carry

    def send_query(i, carry):
        query(i).start()
        return carry

    lax.fori_loop(1, N, send_lin, 0)
    lax.fori_loop(1, N, send_query, 0)
    own_q.wait()
    own_kv.wait()
    fetch_state.wait()

    row8 = lax.broadcasted_iota(jnp.int32, (8, 64), 0)
    lane8 = lax.broadcasted_iota(jnp.int32, (8, 64), 1)
    rates = jnp.sum(jnp.where(lane8 == me * 4 + row8 // 2, rate[...], 0.0), axis=1, keepdims=True)
    second = lax.broadcasted_iota(jnp.int32, (8, 1), 0) % 2 == 1
    lam = jnp.exp(-rates)
    lam_state = jnp.where(second, lam * lam, lam)
    lam_first = jnp.where(second, lam, 1.0)
    lam_second = jnp.where(second, 1.0, 0.0)
    head_of = lax.broadcasted_iota(jnp.int32, (8, WIDTH), 0) // 2

    def spread(x):
        return jnp.concatenate(
            [jnp.broadcast_to(x[:, h * WIDTH:(h + 1) * WIDTH], (2, WIDTH)) for h in range(4)], axis=0
        )

    def lightning(i, carry):
        owner = behind(i)

        @pl.when(i > 0)
        def _():
            a, b = lin_part(i)
            a.wait_recv()
            b.wait_recv()

        for r in range(2):
            request = tab[owner * 2 + r]
            q = lq_in[i, r].astype(jnp.float32)
            q = jnp.concatenate([q[:, h * WIDTH:(h + 1) * WIDTH] for h in range(4)], axis=0)
            kv1 = lkv_in[i, r, 0].astype(jnp.float32)
            kv2 = lkv_in[i, r, 1].astype(jnp.float32)
            q_bf = q.astype(jnp.bfloat16)
            q_two = jnp.concatenate([q_bf, q_bf], axis=1)
            y = jnp.zeros((8, WIDTH), jnp.float32)
            for h in range(4):
                s = state[request, h]
                high = s.astype(jnp.bfloat16)
                low = (s - high.astype(jnp.float32)).astype(jnp.bfloat16)
                got = jnp.dot(q_two, jnp.concatenate([high, low], axis=0), preferred_element_type=jnp.float32)
                y = jnp.where(head_of == h, got, y)
            k1, v1, k2, v2 = spread(kv1[0:1]), spread(kv1[1:2]), spread(kv2[0:1]), spread(kv2[1:2])
            qk1 = jnp.sum(q * k1, axis=1, keepdims=True)
            qk2 = jnp.sum(q * k2, axis=1, keepdims=True)
            y = lam_state * y + (lam_first * qk1) * v1 + (lam_second * qk2) * v2
            norm = jnp.sqrt(jnp.mean(y * y, axis=1, keepdims=True) + 1e-5)
            lin_send[i, r] = y / norm

        @pl.when(i > 0)
        def _():
            lin_back(i).start()

        return carry

    lax.fori_loop(0, N, lightning, 0)
    fetch_pool.wait()

    eye = lax.broadcasted_iota(jnp.int32, (WIDTH, WIDTH), 0) == lax.broadcasted_iota(jnp.int32, (WIDTH, WIDTH), 1)
    position = lax.broadcasted_iota(jnp.int32, (WIDTH, WIDTH), 1)

    def as_row(column):
        return jnp.sum(jnp.where(eye, column, 0.0), axis=0, keepdims=True)

    def softmax(i, carry):
        owner = behind(i)

        @pl.when(i > 0)
        def _():
            query(i).wait_recv()

        found = []
        for k in range(2):
            code = tab[32 + owner * 2 + k]
            page, row, count = code % 16, code // 16 % 2, code // 32
            live = position < count
            q = jnp.where(row == 1, q_all[i, 1], q_all[i, 0])
            scores = jnp.concatenate(
                [
                    lax.dot_general(
                        q[c * 16:(c + 1) * 16], pool[page, 0, :, c * WIDTH:(c + 1) * WIDTH],
                        (((1,), (1,)), ((), ())), preferred_element_type=jnp.float32,
                    )
                    for c in range(KVH)
                ],
                axis=0,
            ) * SCALE
            top = jnp.max(jnp.where(live, scores, LOW), axis=1, keepdims=True)
            weight = jnp.where(live, jnp.exp(scores - top), 0.0)
            total = jnp.sum(weight, axis=1, keepdims=True)
            rounded = weight.astype(jnp.bfloat16)
            acc = jnp.concatenate(
                [
                    jnp.dot(
                        rounded[c * 16:(c + 1) * 16], pool[page, 1, :, c * WIDTH:(c + 1) * WIDTH],
                        preferred_element_type=jnp.float32,
                    )
                    for c in range(KVH)
                ],
                axis=0,
            )
            found.append((row, top, total, acc))
        metas = []
        for r in range(2):
            tops = [jnp.where(row == r, top, LOW) for row, top, _, _ in found]
            peak = jnp.maximum(tops[0], tops[1])
            factors = [
                jnp.where(row == r, jnp.exp(t - peak), 0.0) for t, (row, _, _, _) in zip(tops, found)
            ]
            total = factors[0] * found[0][2] + factors[1] * found[1][2]
            acc = factors[0] * found[0][3] + factors[1] * found[1][3]
            most = jnp.maximum(jnp.max(jnp.abs(acc), axis=1, keepdims=True), 1e-30)
            coded = (acc * (CODES / most) + 32768.5).astype(jnp.int32)
            res_send[i, r] = lax.shift_left(coded[:64], 16) | coded[64:]
            metas += [as_row(peak), as_row(total), as_row(most * (1.0 / CODES))]
        zero = jnp.zeros((2, WIDTH), jnp.float32)
        meta_send[i] = jnp.concatenate(metas + [zero], axis=0)

        @pl.when(i > 0)
        def _():
            result(i).start()
            meta(i).start()

        return carry

    lax.fori_loop(0, N, softmax, 0)

    keep = [
        pltpu.make_async_copy(lin_send.at[0], lin_in.at[me], local_sem.at[4]),
        pltpu.make_async_copy(res_send.at[0], res_in.at[0], local_sem.at[5]),
        pltpu.make_async_copy(meta_send.at[0], meta_in.at[0], local_sem.at[6]),
    ]
    for copy in keep:
        copy.start()

    step = lax.broadcasted_iota(jnp.int32, (WIDTH, 1), 0) % 2

    def by_head(x):
        return jnp.concatenate(
            [jnp.broadcast_to(x[:, c * WIDTH:(c + 1) * WIDTH], (16, WIDTH)) for c in range(KVH)], axis=0
        )

    for r in range(2):
        q = q_all[0, r].astype(jnp.float32)
        kv = [nkv[r, t].astype(jnp.float32) for t in range(2)]
        s0 = jnp.sum(q * by_head(kv[0][0:1]), axis=1, keepdims=True) * SCALE
        s1 = jnp.sum(q * by_head(kv[1][0:1]), axis=1, keepdims=True) * SCALE
        top = jnp.where(step == 1, jnp.maximum(s0, s1), s0)
        w0 = jnp.exp(s0 - top)
        w1 = jnp.where(step == 1, jnp.exp(s1 - top), 0.0)
        r0 = w0.astype(jnp.bfloat16).astype(jnp.float32)
        r1 = w1.astype(jnp.bfloat16).astype(jnp.float32)
        run_acc[r] = r0 * by_head(kv[0][1:2]) + r1 * by_head(kv[1][1:2])
        run_meta[r, 0] = jnp.broadcast_to(top, (WIDTH, WIDTH))
        run_meta[r, 1] = jnp.broadcast_to(w0 + w1, (WIDTH, WIDTH))
    for copy in keep:
        copy.wait()

    def merge(i, carry):
        @pl.when(i > 0)
        def _():
            result(i).wait_recv()
            meta(i).wait_recv()

        columns = jnp.concatenate([meta_in[i], jnp.zeros((WIDTH - 8, WIDTH), jnp.float32)], axis=0).T
        for r in range(2):
            top, total, scale = (columns[:, 3 * r + n:3 * r + n + 1] for n in range(3))
            old = run_meta[r, 0][:, 0:1]
            peak = jnp.maximum(old, top)
            mine, theirs = jnp.exp(old - peak), jnp.exp(top - peak)
            words = res_in[i, r]
            first = lax.shift_right_logical(words, 16).astype(jnp.float32)
            later = (words & 65535).astype(jnp.float32)
            codes = jnp.concatenate([first, later], axis=0) - 32768.0
            run_acc[r] = mine * run_acc[r] + (theirs * scale) * codes
            run_meta[r, 1] = mine * run_meta[r, 1] + theirs * total
            run_meta[r, 0] = jnp.broadcast_to(peak, (WIDTH, WIDTH))
        return carry

    lax.fori_loop(0, N, merge, 0)
    for r in range(2):
        soft_ref[r] = run_acc[r] / run_meta[r, 1]

    def finish(i, carry):
        a, b = lin_part(i)
        a.wait_send()
        b.wait_send()
        query(i).wait_send()
        back = lin_back(i)
        back.wait_send()
        back.wait_recv()
        result(i).wait_send()
        meta(i).wait_send()
        return carry

    lax.fori_loop(1, N, finish, 0)

    def place(i, carry):
        for r in range(2):
            lin_ref[r, pl.ds(pl.multiple_of(i * 8, 8), 8)] = lin_in[i, r]
        return carry

    lax.fori_loop(0, N, place, 0)


def rows_last(x):
    return x.reshape(2, 64, 2, WIDTH).transpose(0, 2, 1, 3).reshape(2, 2, 64 * WIDTH)


def shards(
    request_owner, page_list, context_len, lin_state, decay_rate, lin_query, lin_keyval, soft_query, new_keyval,
    page_pool,
):
    tab = tables(request_owner, page_list, context_len, lax.axis_index("head"))
    vmem = pl.BlockSpec(memory_space=pltpu.VMEM)
    hbm = pl.BlockSpec(memory_space=pl.ANY)
    lin, soft = pl.pallas_call(
        kernel,
        out_shape=[jax.ShapeDtypeStruct((2, WIDTH, WIDTH), jnp.float32)] * 2,
        in_specs=[pl.BlockSpec(memory_space=pltpu.SMEM)] + [vmem] * 5 + [hbm] * 2,
        out_specs=[vmem] * 2,
        scratch_shapes=[
            pltpu.VMEM(lin_state.shape, jnp.float32),
            pltpu.VMEM(page_pool.shape, jnp.bfloat16),
            pltpu.VMEM((N, 2, WIDTH, WIDTH), jnp.bfloat16),
            pltpu.VMEM((N, 2, 2, 512), jnp.bfloat16),
            pltpu.VMEM((N, 2, 2, 2, 512), jnp.bfloat16),
            pltpu.VMEM((N, 2, 8, WIDTH), jnp.float32),
            pltpu.VMEM((N, 2, 8, WIDTH), jnp.float32),
            pltpu.VMEM((N, 2, 64, WIDTH), jnp.int32),
            pltpu.VMEM((N, 2, 64, WIDTH), jnp.int32),
            pltpu.VMEM((N, 8, WIDTH), jnp.float32),
            pltpu.VMEM((N, 8, WIDTH), jnp.float32),
            pltpu.VMEM((2, WIDTH, WIDTH), jnp.float32),
            pltpu.VMEM((2, 2, WIDTH, WIDTH), jnp.float32),
            pltpu.SemaphoreType.DMA((7,)),
            pltpu.SemaphoreType.DMA((6, N)),
            pltpu.SemaphoreType.DMA((6, N)),
        ],
        compiler_params=pltpu.CompilerParams(
            collective_id=0, has_side_effects=True, vmem_limit_bytes=56 * 1024 * 1024
        ),
    )(tab, decay_rate.reshape(1, 64), lin_query, lin_keyval, soft_query, new_keyval, lin_state, page_pool)
    return rows_last(lin), rows_last(soft)


def solution(mesh):
    return jax.shard_map(
        shards,
        mesh=mesh,
        in_specs=(
            P("grp"), P("grp", None), P("grp"), P("grp", "head", None, None), P(),
            P(("grp", "head"), None, None), P(("grp", "head"), None, None, None),
            P(("grp", "head"), None, None), P(("grp", "head"), None, None, None),
            P(("grp", "head"), None, None, None),
        ),
        out_specs=(P(("grp", "head"), None, None), P(("grp", "head"), None, None)),
        check_vma=False,
    )
```

```python
import functools
import math

import jax
import jax.numpy as jnp
from jax import lax
from jax.experimental import pallas as pl
from jax.experimental.pallas import tpu as pltpu
from jax.sharding import PartitionSpec as P

MESH = pl.DeviceIdType.MESH
N = 16
WIDTH = 128
KVH = 8
CODES = 32000.0
LOW = -1e30
SCALE = 1.0 / math.sqrt(128.0)


def offsets(n):
    m = jnp.maximum(n - 7, 0)
    a = jnp.where(n < 4, n - 1, m // 3)
    b = jnp.where(n < 7, n - 4, m % 3)
    dz = jnp.where((n >= 1) & ((n < 4) | (n >= 7)), 1 + 2 * a - 3 * (a // 2), 0)
    dy = jnp.where(n >= 4, 1 + 2 * b - 3 * (b // 2), 0)
    return dz, dy


DIST = (1, 3, 2)
SLOT = {(0, 0): 0}
for _k, _d in enumerate(DIST):
    SLOT[_d, 0] = 1 + _k
    SLOT[0, _d] = 4 + _k
    for _l, _e in enumerate(DIST):
        SLOT[_d, _e] = 7 + 3 * _k + _l


def make_tables(owner, pages, length, me):
    sub = lax.broadcasted_iota(jnp.int32, (32, 32), 0)
    lane = lax.broadcasted_iota(jnp.int32, (32, 32), 1)

    def column(row):
        return jnp.sum(jnp.where(sub == lane, row, 0), axis=1, keepdims=True)

    slot = jnp.sum(jnp.where((column(owner) == owner) & (sub < lane), 1, 0), axis=0, keepdims=True)
    row = owner * 2 + slot
    request_of = jnp.sum(jnp.where(column(row) == lane, sub, 0), axis=0, keepdims=True)
    j = lax.broadcasted_iota(jnp.int32, (8, 32), 0)
    count = jnp.clip(length - j * WIDTH, 0, WIDTH)
    here = (lax.shift_right_logical(pages, 4) == me) & (count > 0)
    code = (pages & 15) + count * 16
    least = jnp.min(jnp.where(here, j, 8), axis=0, keepdims=True)
    most = jnp.max(jnp.where(here, j, -1), axis=0, keepdims=True)
    first = jnp.sum(jnp.where(here & (j == least), code, 0), axis=0, keepdims=True)
    second = jnp.sum(jnp.where(here & (j == most) & (most != least), code, 0), axis=0, keepdims=True)
    return request_of, first, second


def kernel(
    owner, pages, length, rate, sq, nkv, lq, lkv, state_hbm, pool_hbm, lin_ref, soft_ref,
    state, pool, q_all, lq_mid, lkv_mid, lq_in, lkv_in, lin_send, lin_in, res_send, res_in, meta_send, meta_in,
    run_acc, run_meta, tab_rows, tab, local_sem, half_send, half_recv, mid_send, mid_recv, back_send, back_recv,
):
    me = lax.axis_index("head")
    mz, my = me // 4, me % 4

    def at_offset(dz, dy):
        return (mz + dz) % 4 * 4 + (my + dy) % 4

    def behind(n):
        dz, dy = offsets(n)
        return at_offset(4 - dz, 4 - dy)

    def remote(src, dst, send, recv, to):
        return pltpu.make_async_remote_copy(
            src_ref=src, dst_ref=dst, send_sem=send, recv_sem=recv, device_id={"head": to}, device_id_type=MESH
        )

    def half(h, src, dst, to):
        part = pl.ds(64 * h, 64)
        return remote(
            q_all.at[src, :, part], q_all.at[dst, :, part], half_send.at[h, dst], half_recv.at[h, dst], to
        )

    def lin_back(n):
        mine = pl.ds(pl.multiple_of(me * 8, 8), 8)
        return remote(lin_send.at[n], lin_in.at[:, mine], back_send.at[0, n], back_recv.at[0, n], behind(n))

    def back(n):
        to = behind(n)
        return (
            remote(res_send.at[n], res_in.at[n], back_send.at[1, n], back_recv.at[1, n], to),
            remote(meta_send.at[n], meta_in.at[n], back_send.at[2, n], back_recv.at[2, n], to),
        )

    barrier = pltpu.get_barrier_semaphore()
    for d in DIST:
        for to in (at_offset(d, 0), at_offset(0, d)):
            pl.semaphore_signal(barrier, inc=1, device_id={"head": to}, device_id_type=MESH)
    fetch_state = pltpu.make_async_copy(state_hbm, state, local_sem.at[0])
    fetch_pool = pltpu.make_async_copy(pool_hbm, pool, local_sem.at[1])
    fetch_state.start()
    fetch_pool.start()

    def wide(dz):
        return pl.ds(pl.multiple_of((mz + dz) % 4 * 2048, 2048), 2048)

    def narrow(dy):
        return pl.ds(pl.multiple_of((my + dy) % 4 * 512, 512), 512)

    own_mid = [
        pltpu.make_async_copy(lq.at[:, :, wide(0)], lq_mid.at[0], local_sem.at[2]),
        pltpu.make_async_copy(lkv.at[:, :, :, wide(0)], lkv_mid.at[0], local_sem.at[3]),
    ]
    for copy in own_mid:
        copy.start()
    for r in range(2):
        q_all[0, r] = sq[r].astype(jnp.float32).T.astype(jnp.bfloat16)
    tab_rows[...] = jnp.zeros((8, WIDTH), jnp.int32)
    for n, row in enumerate(make_tables(owner[...], pages[...], length[...], me)):
        tab_rows[n:n + 1, 0:32] = row
    fill_tab = pltpu.make_async_copy(tab_rows, tab, local_sem.at[4])
    fill_tab.start()
    pl.semaphore_wait(barrier, 6)

    mids = []
    for k, d in enumerate(DIST):
        to = at_offset(d, 0)
        mids.append(remote(lq.at[:, :, wide(d)], lq_mid.at[d], mid_send.at[0, d], mid_recv.at[0, d], to))
        mids.append(remote(lkv.at[:, :, :, wide(d)], lkv_mid.at[d], mid_send.at[1, d], mid_recv.at[1, d], to))
    for copy in mids:
        copy.start()

    first = {}
    for d in DIST:
        first[0, d] = half(0, 0, SLOT[d, 0], at_offset(d, 0))
        first[1, d] = half(1, 0, SLOT[0, d], at_offset(0, d))
    for copy in first.values():
        copy.start()
    for d in DIST:
        half(0, 0, SLOT[0, d], at_offset(0, d)).start()
        half(1, 0, SLOT[d, 0], at_offset(d, 0)).start()
    for copy in own_mid:
        copy.wait()
    for d in DIST:
        first[0, d].wait_recv()
        for e in DIST:
            half(0, SLOT[d, 0], SLOT[d, e], at_offset(0, e)).start()
        first[1, d].wait_recv()
        for e in DIST:
            half(1, SLOT[0, d], SLOT[e, d], at_offset(e, 0)).start()
    for copy in mids:
        copy.wait_recv()
    lasts = []
    for d in DIST:
        to = at_offset(0, d)
        lasts.append(remote(lq_mid.at[:, :, :, narrow(d)], lq_in.at[d], mid_send.at[2, d], mid_recv.at[2, d], to))
        lasts.append(remote(lkv_mid.at[:, :, :, :, narrow(d)], lkv_in.at[d], mid_send.at[3, d], mid_recv.at[3, d], to))
    for copy in lasts:
        copy.start()
    own_last = [
        pltpu.make_async_copy(lq_mid.at[:, :, :, narrow(0)], lq_in.at[0], local_sem.at[2]),
        pltpu.make_async_copy(lkv_mid.at[:, :, :, :, narrow(0)], lkv_in.at[0], local_sem.at[3]),
    ]
    for copy in own_last:
        copy.start()

    row8 = lax.broadcasted_iota(jnp.int32, (8, 64), 0)
    lane8 = lax.broadcasted_iota(jnp.int32, (8, 64), 1)
    rates = jnp.sum(jnp.where(lane8 == me * 4 + row8 // 2, rate[...], 0.0), axis=1, keepdims=True)
    second = lax.broadcasted_iota(jnp.int32, (8, 1), 0) % 2 == 1
    lam = jnp.exp(-rates)
    lam_state = jnp.where(second, lam * lam, lam)
    lam_first = jnp.where(second, lam, 1.0)
    lam_second = jnp.where(second, 1.0, 0.0)
    head_of = lax.broadcasted_iota(jnp.int32, (8, WIDTH), 0) // 2

    def spread(x):
        return jnp.concatenate(
            [jnp.broadcast_to(x[:, h * WIDTH:(h + 1) * WIDTH], (2, WIDTH)) for h in range(4)], axis=0
        )

    def lightning(n):
        dz, dy = offsets(n)
        owner_at = behind(n)
        for r in range(2):
            request = tab[0, owner_at * 2 + r] & 31
            q = lq_in[dy, dz, r].astype(jnp.float32)
            q = jnp.concatenate([q[:, h * WIDTH:(h + 1) * WIDTH] for h in range(4)], axis=0)
            kv1 = lkv_in[dy, dz, r, 0].astype(jnp.float32)
            kv2 = lkv_in[dy, dz, r, 1].astype(jnp.float32)
            q_bf = q.astype(jnp.bfloat16)
            q_two = jnp.concatenate([q_bf, q_bf], axis=1)
            y = jnp.zeros((8, WIDTH), jnp.float32)
            for h in range(4):
                s = state[request, h]
                high = s.astype(jnp.bfloat16)
                low = (s - high.astype(jnp.float32)).astype(jnp.bfloat16)
                got = jnp.dot(q_two, jnp.concatenate([high, low], axis=0), preferred_element_type=jnp.float32)
                y = jnp.where(head_of == h, got, y)
            k1, v1, k2, v2 = spread(kv1[0:1]), spread(kv1[1:2]), spread(kv2[0:1]), spread(kv2[1:2])
            qk1 = jnp.sum(q * k1, axis=1, keepdims=True)
            qk2 = jnp.sum(q * k2, axis=1, keepdims=True)
            y = lam_state * y + (lam_first * qk1) * v1 + (lam_second * qk2) * v2
            norm = jnp.sqrt(jnp.mean(y * y, axis=1, keepdims=True) + 1e-5)
            lin_send[n, r] = y / norm

    position = lax.broadcasted_iota(jnp.int32, (WIDTH, WIDTH), 0)
    lane_head = lax.broadcasted_iota(jnp.int32, (WIDTH, WIDTH), 1) // 16
    of_head = [jnp.where(lane_head == c, 1.0, 0.0).astype(jnp.bfloat16) for c in range(KVH)]

    def page_part(page, count, q):
        scores = sum(
            jnp.dot(
                pool[page, 0, :, c * WIDTH:(c + 1) * WIDTH], q * of_head[c], preferred_element_type=jnp.float32
            )
            for c in range(KVH)
        ) * SCALE
        live = position < count
        top = jnp.max(jnp.where(live, scores, LOW), axis=0, keepdims=True)
        weight = jnp.where(live, jnp.exp(scores - top), 0.0)
        total = jnp.sum(weight, axis=0, keepdims=True)
        rounded = weight.astype(jnp.bfloat16)
        acc = sum(
            lax.dot_general(
                pool[page, 1, :, c * WIDTH:(c + 1) * WIDTH], rounded * of_head[c], (((0,), (0,)), ((), ())),
                preferred_element_type=jnp.float32,
            )
            for c in range(KVH)
        )
        return top, total, acc

    def softmax(n):
        owner_at = behind(n)
        a, b = tab[0, owner_at * 2] & 31, tab[0, owner_at * 2 + 1] & 31
        first_a, second_a, first_b, second_b = tab[1, a], tab[2, a], tab[1, b], tab[2, b]
        codes = (
            jnp.where(first_a > 0, first_a, first_b),
            jnp.where(second_a > 0, second_a, jnp.where(first_a > 0, first_b, second_b)),
        )
        rows = (jnp.where(first_a > 0, 0, 1), jnp.where(second_a > 0, 0, 1))
        found = []
        for code, row in zip(codes, rows):
            q = jnp.where(row == 1, q_all[n, 1], q_all[n, 0])
            found.append((row, *page_part(code & 15, lax.shift_right_logical(code, 4), q)))
        metas = []
        for r in range(2):
            tops = [jnp.where(row == r, top, LOW) for row, top, _, _ in found]
            peak = jnp.maximum(tops[0], tops[1])
            factors = [jnp.where(row == r, jnp.exp(t - peak), 0.0) for t, (row, _, _, _) in zip(tops, found)]
            total = factors[0] * found[0][2] + factors[1] * found[1][2]
            acc = factors[0] * found[0][3] + factors[1] * found[1][3]
            most = jnp.maximum(jnp.max(jnp.abs(acc), axis=0, keepdims=True), 1e-30)
            coded = (acc * (CODES / most) + 32768.5).astype(jnp.int32)
            res_send[n, r] = lax.shift_left(coded[:64], 16) | coded[64:]
            metas += [peak, total, most * (1.0 / CODES)]
        meta_send[n] = jnp.concatenate(metas + [jnp.zeros((2, WIDTH), jnp.float32)], axis=0)

    fetch_pool.wait()
    fill_tab.wait()
    def lightning_pair(p, carry):
        for n in (2 * p, 2 * p + 1):
            lightning(n)
        for n in (2 * p, 2 * p + 1):

            @pl.when(n > 0)
            def _(n=n):
                lin_back(n).start()

        return carry

    def pair(p, carry):
        @pl.when(p == 4)
        def _():
            for copy in own_last:
                copy.wait()
            for copy in lasts:
                copy.wait_recv()
            fetch_state.wait()
            lax.fori_loop(0, 8, lightning_pair, 0)

        for n in (2 * p, 2 * p + 1):

            @pl.when(n >= 4)
            def _(n=n):
                half(0, 0, n, at_offset(1, 0)).wait_recv()

            @pl.when((n >= 7) | ((n >= 1) & (n < 4)))
            def _(n=n):
                half(1, 0, n, at_offset(1, 0)).wait_recv()

        for n in (2 * p, 2 * p + 1):
            softmax(n)
        for n in (2 * p, 2 * p + 1):

            @pl.when(n > 0)
            def _(n=n):
                for copy in back(n):
                    copy.start()

        return carry

    lax.fori_loop(0, 8, pair, 0)
    keep = pltpu.make_async_copy(
        lin_send.at[0], lin_in.at[:, pl.ds(pl.multiple_of(me * 8, 8), 8)], local_sem.at[5]
    )
    keep.start()

    step = lax.broadcasted_iota(jnp.int32, (1, WIDTH), 1) % 2

    def by_head(x):
        return jnp.concatenate(
            [jnp.broadcast_to(x[:, c * WIDTH:(c + 1) * WIDTH], (16, WIDTH)) for c in range(KVH)], axis=0
        ).T

    def merge_in(acc, peak_old, total, r, sources):
        peak = peak_old
        for meta, _ in sources:
            peak = jnp.maximum(peak, meta[3 * r:3 * r + 1])
        keep_factor = jnp.exp(peak_old - peak)
        total = total * keep_factor
        factors = []
        shift = jnp.zeros((1, WIDTH), jnp.float32)
        for meta, _ in sources:
            factor = jnp.exp(meta[3 * r:3 * r + 1] - peak)
            total = total + factor * meta[3 * r + 1:3 * r + 2]
            factors.append(factor * meta[3 * r + 2:3 * r + 3])
            shift = shift + factors[-1] * 32768.0
        upper = acc[:64] * keep_factor - shift
        lower = acc[64:] * keep_factor - shift
        for factor, (_, words) in zip(factors, sources):
            upper = upper + factor * lax.shift_right_logical(words, 16).astype(jnp.float32)
            lower = lower + factor * (words & 65535).astype(jnp.float32)
        return jnp.concatenate([upper, lower], axis=0), peak, total

    def keep_run(r, acc, peak, total):
        run_acc[r] = acc
        run_meta[r, 0:1] = peak
        run_meta[r, 1:2] = total

    for r in range(2):
        q = q_all[0, r].astype(jnp.float32)
        kv = [nkv[r, t].astype(jnp.float32) for t in range(2)]
        s0 = jnp.sum(q * by_head(kv[0][0:1]), axis=0, keepdims=True) * SCALE
        s1 = jnp.sum(q * by_head(kv[1][0:1]), axis=0, keepdims=True) * SCALE
        top = jnp.where(step == 1, jnp.maximum(s0, s1), s0)
        w0 = jnp.exp(s0 - top)
        w1 = jnp.where(step == 1, jnp.exp(s1 - top), 0.0)
        r0 = w0.astype(jnp.bfloat16).astype(jnp.float32)
        r1 = w1.astype(jnp.bfloat16).astype(jnp.float32)
        acc = r0 * by_head(kv[0][1:2]) + r1 * by_head(kv[1][1:2])
        keep_run(r, *merge_in(acc, top, w0 + w1, r, [(meta_send[0], res_send[0, r])]))

    def merge(p, carry):
        slots = [3 * p + 1 + k for k in range(3)]
        for n in slots:
            for copy in back(n):
                copy.wait_recv()
        for r in range(2):
            sources = [(meta_in[n], res_in[n, r]) for n in slots]
            keep_run(r, *merge_in(run_acc[r], run_meta[r, 0:1], run_meta[r, 1:2], r, sources))
        return carry

    lax.fori_loop(0, 5, merge, 0)
    for r in range(2):
        soft_ref[r] = (run_acc[r] / run_meta[r, 1:2]).T

    def finish(n, carry):
        half(0, 0, n, at_offset(1, 0)).wait_send()
        half(1, 0, n, at_offset(1, 0)).wait_send()
        lin = lin_back(n)
        lin.wait_recv()
        lin.wait_send()
        for copy in back(n):
            copy.wait_send()
        return carry

    lax.fori_loop(1, N, finish, 0)
    for copy in mids + lasts:
        copy.wait_send()
    keep.wait()
    lin_ref[...] = lin_in[...]


def copy_kernel(a_ref, b_ref, c_ref, d_ref):
    c_ref[...] = a_ref[...]
    d_ref[...] = b_ref[...]


def rows_first(x):
    return x.reshape(2, 2, 64, WIDTH).transpose(0, 2, 1, 3).reshape(2, WIDTH, WIDTH)


def rows_last(x):
    return x.reshape(2, 64, 2, WIDTH).transpose(0, 2, 1, 3).reshape(2, 2, 64 * WIDTH)


def shards(
    request_owner, page_list, context_len, lin_state, decay_rate, lin_query, lin_keyval, soft_query, new_keyval,
    page_pool,
):
    vmem = pl.BlockSpec(memory_space=pltpu.VMEM)
    hbm = pl.BlockSpec(memory_space=pl.ANY)
    out = [jax.ShapeDtypeStruct((2, WIDTH, WIDTH), jnp.float32)] * 2
    lin, soft = pl.pallas_call(
        kernel,
        out_shape=out,
        in_specs=[vmem] * 6 + [hbm] * 4,
        out_specs=[vmem] * 2,
        scratch_shapes=[
            pltpu.VMEM(lin_state.shape, jnp.float32),
            pltpu.VMEM(page_pool.shape, jnp.bfloat16),
            pltpu.VMEM((N, 2, WIDTH, WIDTH), jnp.bfloat16),
            pltpu.VMEM((4, 2, 2, 2048), jnp.bfloat16),
            pltpu.VMEM((4, 2, 2, 2, 2048), jnp.bfloat16),
            pltpu.VMEM((4, 4, 2, 2, 512), jnp.bfloat16),
            pltpu.VMEM((4, 4, 2, 2, 2, 512), jnp.bfloat16),
            pltpu.VMEM((N, 2, 8, WIDTH), jnp.float32),
            pltpu.VMEM((2, WIDTH, WIDTH), jnp.float32),
            pltpu.VMEM((N, 2, 64, WIDTH), jnp.int32),
            pltpu.VMEM((N, 2, 64, WIDTH), jnp.int32),
            pltpu.VMEM((N, 8, WIDTH), jnp.float32),
            pltpu.VMEM((N, 8, WIDTH), jnp.float32),
            pltpu.VMEM((2, WIDTH, WIDTH), jnp.float32),
            pltpu.VMEM((2, 8, WIDTH), jnp.float32),
            pltpu.VMEM((8, WIDTH), jnp.int32),
            pltpu.SMEM((8, WIDTH), jnp.int32),
            pltpu.SemaphoreType.DMA((6,)),
            pltpu.SemaphoreType.DMA((2, N)),
            pltpu.SemaphoreType.DMA((2, N)),
            pltpu.SemaphoreType.DMA((4, 4)),
            pltpu.SemaphoreType.DMA((4, 4)),
            pltpu.SemaphoreType.DMA((3, N)),
            pltpu.SemaphoreType.DMA((3, N)),
        ],
        compiler_params=pltpu.CompilerParams(
            collective_id=0, has_side_effects=True, vmem_limit_bytes=56 * 1024 * 1024
        ),
    )(
        request_owner.reshape(1, 32), page_list.T, context_len.reshape(1, 32), decay_rate.reshape(1, 64),
        rows_first(soft_query), new_keyval, lin_query, lin_keyval, lin_state, page_pool,
    )
    lin, soft = pl.pallas_call(copy_kernel, out_shape=out, in_specs=[vmem] * 2, out_specs=[vmem] * 2)(lin, soft)
    return rows_last(lin), rows_last(soft)


def solution(mesh):
    return jax.shard_map(
        shards,
        mesh=mesh,
        in_specs=(
            P("grp"), P("grp", None), P("grp"), P("grp", "head", None, None), P(),
            P(("grp", "head"), None, None), P(("grp", "head"), None, None, None),
            P(("grp", "head"), None, None), P(("grp", "head"), None, None, None),
            P(("grp", "head"), None, None, None),
        ),
        out_specs=(P(("grp", "head"), None, None), P(("grp", "head"), None, None)),
        check_vma=False,
    )
```

```python
import functools
import math

import jax
import jax.numpy as jnp
from jax import lax
from jax.experimental import pallas as pl
from jax.experimental.pallas import tpu as pltpu
from jax.sharding import PartitionSpec as P

MESH = pl.DeviceIdType.MESH
N = 16
WIDTH = 128
KVH = 8
CODES = 32000.0
LOW = -1e30
NONE = -505.0
LEVEL_UNIT = 2.0**22
SIZE_UNIT = 2.0**16
SCALE = 1.0 / math.sqrt(128.0)


DIST = (1, 3, 2)
OFFSETS = ((0, 0), (1, 0), (0, 1), (3, 0), (0, 3), (2, 0), (0, 2), (1, 1), (1, 3), (3, 1), (3, 3), (1, 2), (2, 1), (3, 2), (2, 3), (2, 2))
SLOT = {offset: n for n, offset in enumerate(OFFSETS)}


def offsets(n):
    return tuple(
        sum(jnp.where(n == i, offset[axis], 0) for i, offset in enumerate(OFFSETS) if offset[axis]) for axis in (0, 1)
    )


def make_tables(owner, pages, length, me):
    sub = lax.broadcasted_iota(jnp.int32, (32, 32), 0)
    lane = lax.broadcasted_iota(jnp.int32, (32, 32), 1)

    def column(row):
        return jnp.sum(jnp.where(sub == lane, row, 0), axis=1, keepdims=True)

    slot = jnp.sum(jnp.where((column(owner) == owner) & (sub < lane), 1, 0), axis=0, keepdims=True)
    row = owner * 2 + slot
    request_of = jnp.sum(jnp.where(column(row) == lane, sub, 0), axis=0, keepdims=True)
    j = lax.broadcasted_iota(jnp.int32, (8, 32), 0)
    count = jnp.clip(length - j * WIDTH, 0, WIDTH)
    here = (lax.shift_right_logical(pages, 4) == me) & (count > 0)
    code = (pages & 15) + count * 16
    least = jnp.min(jnp.where(here, j, 8), axis=0, keepdims=True)
    most = jnp.max(jnp.where(here, j, -1), axis=0, keepdims=True)
    first = jnp.sum(jnp.where(here & (j == least), code, 0), axis=0, keepdims=True)
    second = jnp.sum(jnp.where(here & (j == most) & (most != least), code, 0), axis=0, keepdims=True)
    return request_of, first, second


def kernel(
    owner, pages, length, rate, sq_hbm, nkv_hbm, lq_hbm, lkv_hbm, state_hbm, pool_hbm, lin_ref, soft_ref,
    state, pool, sq, nkv, lq, lkv, lin_fresh, lin_out, q_all, lin_pack, lin_mid, lin_all, lin_send, lin_in, part_send, part_in, mid_send, mid_in,
    tab_rows, tab, local_sem, half_send, half_recv, mid_sems, mid_recvs, back_send, back_recv,
    part_sems, part_recvs, last_sems, last_recvs,
):
    me = lax.axis_index("head")
    mz, my = me // 4, me % 4

    def at_offset(dz, dy):
        return (mz + dz) % 4 * 4 + (my + dy) % 4

    def behind(n):
        dz, dy = offsets(n)
        return at_offset(4 - dz, 4 - dy)

    def remote(src, dst, send, recv, to):
        return pltpu.make_async_remote_copy(
            src_ref=src, dst_ref=dst, send_sem=send, recv_sem=recv, device_id={"head": to}, device_id_type=MESH
        )

    def half(h, src, dst, to):
        rows = pl.ds(64 * h, 64)
        return remote(
            q_all.at[src, :, rows], q_all.at[dst, :, rows], half_send.at[h, dst], half_recv.at[h, dst], to
        )

    def lin_back(n):
        return remote(lin_send.at[n], lin_in.at[n], back_send.at[n], back_recv.at[n], behind(n))

    def part(h, dz, dy):
        to = at_offset(4 - dz, 0) if h == 0 else at_offset(0, 4 - dy)
        n = dz * 4 + dy
        return remote(part_send.at[h, n], part_in.at[h, n], part_sems.at[h, n], part_recvs.at[h, n], to)

    def last(h, d):
        to = at_offset(0, 4 - d) if h == 0 else at_offset(4 - d, 0)
        return remote(mid_send.at[h, d], mid_in.at[h, d], last_sems.at[h, d], last_recvs.at[h, d], to)

    barrier = pltpu.get_barrier_semaphore()
    for d in DIST:
        for to in (at_offset(d, 0), at_offset(0, d)):
            pl.semaphore_signal(barrier, inc=1, device_id={"head": to}, device_id_type=MESH)
    loads = [
        pltpu.make_async_copy(src, dst, local_sem.at[5 + n])
        for n, (src, dst) in enumerate(((sq_hbm, sq), (lq_hbm, lq), (lkv_hbm, lkv), (nkv_hbm, nkv)))
    ]
    for copy in loads:
        copy.start()
    fetch_pool = pltpu.make_async_copy(pool_hbm, pool, local_sem.at[1])
    fetch_state = pltpu.make_async_copy(state_hbm, state, local_sem.at[0])
    fetch_pool.start()
    fetch_state.start()
    tab_rows[...] = jnp.zeros((8, WIDTH), jnp.int32)
    for n, row in enumerate(make_tables(owner[...], pages[...], length[...], me)):
        tab_rows[n:n + 1, 0:32] = row
    fill_tab = pltpu.make_async_copy(tab_rows, tab, local_sem.at[4])
    fill_tab.start()
    for copy in loads:
        copy.wait()
    wide = [lq[r].astype(jnp.float32) for r in range(2)]
    for peer in range(N):
        lin_pack[peer // 4, peer % 4] = jnp.concatenate(
            [x[peer * 8:peer * 8 + 8] for x in wide], axis=0
        ).astype(jnp.bfloat16)
    own_mid = pltpu.make_async_copy(lin_pack.at[mz], lin_mid.at[0], local_sem.at[2])
    own_mid.start()
    for r in range(2):
        q_all[0, r] = sq[r].astype(jnp.float32).T.astype(jnp.bfloat16)

    row_of = lax.broadcasted_iota(jnp.int32, (WIDTH, 64), 0)
    lane_of = lax.broadcasted_iota(jnp.int32, (WIDTH, 64), 1)
    rates = jnp.sum(jnp.where(lane_of == row_of // 2, rate[...], 0.0), axis=1, keepdims=True)
    second = lax.broadcasted_iota(jnp.int32, (WIDTH, 1), 0) % 2 == 1
    lam = jnp.exp(-rates)
    lam_state = jnp.where(second, lam * lam, lam)
    lam_first = jnp.where(second, lam, 1.0)
    lam_second = jnp.where(second, 1.0, 0.0)
    odd = lax.broadcasted_iota(jnp.int32, (WIDTH, WIDTH), 0) % 2 == 1

    def keys_values(x):
        return jnp.where(odd, pltpu.roll(x, 1, 0), x), jnp.where(odd, x, pltpu.roll(x, WIDTH - 1, 0))

    for r in range(2):
        k1, v1 = keys_values(lkv[r, 0].astype(jnp.float32))
        k2, v2 = keys_values(lkv[r, 1].astype(jnp.float32))
        qk1 = jnp.sum(wide[r] * k1, axis=1, keepdims=True)
        qk2 = jnp.sum(wide[r] * k2, axis=1, keepdims=True)
        lin_fresh[r] = (lam_first * qk1) * v1 + (lam_second * qk2) * v2
    lin_fresh[2] = jnp.broadcast_to(lam_state, (WIDTH, WIDTH))
    pl.semaphore_wait(barrier, 6)

    mids = [
        remote(lin_pack.at[(mz + d) % 4], lin_mid.at[d], mid_sems.at[0, d], mid_recvs.at[0, d], at_offset(d, 0))
        for d in DIST
    ]
    for copy in mids:
        copy.start()

    first = {}
    for d in DIST:
        first[0, d] = half(0, 0, SLOT[d, 0], at_offset(d, 0))
        first[1, d] = half(1, 0, SLOT[0, d], at_offset(0, d))
    for copy in first.values():
        copy.start()
    for d in DIST:
        half(0, 0, SLOT[0, d], at_offset(0, d)).start()
        half(1, 0, SLOT[d, 0], at_offset(d, 0)).start()
    own_mid.wait()
    for copy in mids:
        copy.wait_recv()
    lasts = [
        remote(
            lin_mid.at[:, (my + d) % 4], lin_all.at[d], mid_sems.at[1, d], mid_recvs.at[1, d], at_offset(0, d)
        )
        for d in DIST
    ]
    for copy in lasts:
        copy.start()
    own_last = pltpu.make_async_copy(lin_mid.at[:, my], lin_all.at[0], local_sem.at[3])
    own_last.start()
    for d in DIST:
        first[0, d].wait_recv()
        for e in DIST:
            half(0, SLOT[d, 0], SLOT[d, e], at_offset(0, e)).start()
        first[1, d].wait_recv()
        for e in DIST:
            half(1, SLOT[0, d], SLOT[e, d], at_offset(e, 0)).start()

    head_of = lax.broadcasted_iota(jnp.int32, (8, WIDTH), 0) // 2

    def lightning(n):
        dz, dy = offsets(n)
        owner_at = behind(n)
        block = lin_all[dy, dz].astype(jnp.float32)
        for r in range(2):
            request = tab[0, owner_at * 2 + r] & 31
            q = block[8 * r:8 * r + 8].astype(jnp.bfloat16)
            q_two = jnp.concatenate([q, q], axis=1)
            y = jnp.zeros((8, WIDTH), jnp.float32)
            for h in range(4):
                s = state[request, h]
                high = s.astype(jnp.bfloat16)
                low = (s - high.astype(jnp.float32)).astype(jnp.bfloat16)
                got = jnp.dot(q_two, jnp.concatenate([high, low], axis=0), preferred_element_type=jnp.float32)
                y = jnp.where(head_of == h, got, y)
            lin_send[n, r] = y

    position = lax.broadcasted_iota(jnp.int32, (WIDTH, WIDTH), 0)
    lane_head = lax.broadcasted_iota(jnp.int32, (WIDTH, WIDTH), 1) // 16
    of_head = [jnp.where(lane_head == c, 1.0, 0.0).astype(jnp.bfloat16) for c in range(KVH)]

    def page_part(page, count, q):
        scores = sum(
            jnp.dot(
                pool[page, 0, :, c * WIDTH:(c + 1) * WIDTH], q * of_head[c], preferred_element_type=jnp.float32
            )
            for c in range(KVH)
        ) * SCALE
        live = position < count
        top = jnp.max(jnp.where(live, scores, LOW), axis=0, keepdims=True)
        weight = jnp.where(live, jnp.exp(scores - top), 0.0)
        total = jnp.sum(weight, axis=0, keepdims=True)
        rounded = weight.astype(jnp.bfloat16)
        acc = sum(
            lax.dot_general(
                pool[page, 1, :, c * WIDTH:(c + 1) * WIDTH], rounded * of_head[c], (((0,), (0,)), ((), ())),
                preferred_element_type=jnp.float32,
            )
            for c in range(KVH)
        )
        return top, total, acc

    def encode(found):
        words, logs = [], []
        for upper, lower, level in found:
            most = jnp.maximum(
                jnp.max(jnp.abs(upper), axis=0, keepdims=True), jnp.max(jnp.abs(lower), axis=0, keepdims=True)
            )
            size = jnp.ceil(jnp.log(jnp.maximum(most, 1e-30)) * SIZE_UNIT)
            inverse = CODES * jnp.exp(size * (-1.0 / SIZE_UNIT))
            high = (upper * inverse + 32768.5).astype(jnp.int32)
            low = (lower * inverse + 32768.5).astype(jnp.int32)
            words.append(lax.shift_left(high, 16) | low)
            logs += [(level * LEVEL_UNIT).astype(jnp.int32), size.astype(jnp.int32)]
        return jnp.concatenate(words + logs + [jnp.zeros((4, WIDTH), jnp.int32)], axis=0)

    def merged(sources, r, more=None):
        levels = [x[64 + 2 * r:65 + 2 * r].astype(jnp.float32) * (1.0 / LEVEL_UNIT) for x in sources]
        sizes = [x[65 + 2 * r:66 + 2 * r].astype(jnp.float32) * (1.0 / SIZE_UNIT) for x in sources]
        peak = functools.reduce(jnp.maximum, levels + ([more[2]] if more else []))
        weights = [jnp.where(x > NONE + 20.0, jnp.exp(x - peak), 0.0) for x in levels]
        total = sum(weights)
        factors = [w * jnp.exp(size) * (1.0 / CODES) for w, size in zip(weights, sizes)]
        shift = sum(factors) * 32768.0
        upper, lower = -shift, -shift
        if more:
            weight = jnp.exp(more[2] - peak)
            total = total + weight
            upper, lower = weight * more[0] - shift, weight * more[1] - shift
        for factor, x in zip(factors, sources):
            words = x[32 * r:32 * r + 32]
            upper = upper + factor * lax.shift_right_logical(words, 16).astype(jnp.float32)
            lower = lower + factor * (words & 65535).astype(jnp.float32)
        total = jnp.maximum(total, 1e-30)
        inverse = 1.0 / total
        return upper * inverse, lower * inverse, jnp.maximum(peak + jnp.log(total), NONE)

    def softmax(n):
        dz, dy = offsets(n)
        owner_at = behind(n)
        a, b = tab[0, owner_at * 2] & 31, tab[0, owner_at * 2 + 1] & 31
        first_a, second_a, first_b, second_b = tab[1, a], tab[2, a], tab[1, b], tab[2, b]
        codes = (
            jnp.where(first_a > 0, first_a, first_b),
            jnp.where(second_a > 0, second_a, jnp.where(first_a > 0, first_b, second_b)),
        )
        rows = (jnp.where(first_a > 0, 0, 1), jnp.where(second_a > 0, 0, 1))
        found = []
        for code, row in zip(codes, rows):
            q = jnp.where(row == 1, q_all[n, 1], q_all[n, 0])
            found.append((row, *page_part(code & 15, lax.shift_right_logical(code, 4), q)))
        values = []
        for r in range(2):
            tops = [jnp.where(row == r, top, LOW) for row, top, _, _ in found]
            peak = jnp.maximum(tops[0], tops[1])
            factors = [jnp.where(row == r, jnp.exp(t - peak), 0.0) for t, (row, _, _, _) in zip(tops, found)]
            total = jnp.maximum(factors[0] * found[0][2] + factors[1] * found[1][2], 1e-30)
            inverse = 1.0 / total
            value = (factors[0] * inverse) * found[0][3] + (factors[1] * inverse) * found[1][3]
            values.append((value, jnp.maximum(peak + jnp.log(total), NONE)))
        for h in range(2):
            part_send[h, dz * 4 + dy] = encode(
                [(v[32 * h:32 * h + 32], v[64 + 32 * h:96 + 32 * h], level) for v, level in values]
            )

    fetch_pool.wait()
    fill_tab.wait()

    def lightning_pair(p, carry):
        for n in (2 * p, 2 * p + 1):
            lightning(n)
        for n in (2 * p, 2 * p + 1):

            @pl.when(n > 0)
            def _(n=n):
                lin_back(n).start()

        return carry

    def pair(p, carry):
        for n in (2 * p, 2 * p + 1):
            dz, dy = offsets(n)

            @pl.when(dy > 0)
            def _(n=n):
                half(0, 0, n, at_offset(1, 0)).wait_recv()

            @pl.when(dz > 0)
            def _(n=n):
                half(1, 0, n, at_offset(1, 0)).wait_recv()

        for n in (2 * p, 2 * p + 1):
            softmax(n)
        for n in (2 * p, 2 * p + 1):
            dz, dy = offsets(n)

            @pl.when(dz > 0)
            def _(dz=dz, dy=dy):
                part(0, dz, dy).start()

            @pl.when(dy > 0)
            def _(dz=dz, dy=dy):
                part(1, dz, dy).start()

        return carry

    lax.fori_loop(0, 8, pair, 0)
    own_last.wait()
    for copy in lasts:
        copy.wait_recv()
    fetch_state.wait()
    lax.fori_loop(0, 8, lightning_pair, 0)

    step = lax.broadcasted_iota(jnp.int32, (1, WIDTH), 1) % 2

    def by_head(x):
        return jnp.concatenate(
            [jnp.broadcast_to(x[:, c * WIDTH:(c + 1) * WIDTH], (16, WIDTH)) for c in range(KVH)], axis=0
        ).T

    fresh = []
    for r in range(2):
        q = q_all[0, r].astype(jnp.float32)
        kv = [nkv[r, t].astype(jnp.float32) for t in range(2)]
        s0 = jnp.sum(q * by_head(kv[0][0:1]), axis=0, keepdims=True) * SCALE
        s1 = jnp.sum(q * by_head(kv[1][0:1]), axis=0, keepdims=True) * SCALE
        top = jnp.where(step == 1, jnp.maximum(s0, s1), s0)
        w0 = jnp.exp(s0 - top)
        w1 = jnp.where(step == 1, jnp.exp(s1 - top), 0.0)
        r0 = w0.astype(jnp.bfloat16).astype(jnp.float32)
        r1 = w1.astype(jnp.bfloat16).astype(jnp.float32)
        value = (r0 * by_head(kv[0][1:2]) + r1 * by_head(kv[1][1:2])) / (w0 + w1)
        fresh.append((value, top + jnp.log(w0 + w1)))

    def middle(k, carry):
        d = jnp.where(k < 3, 1 + 2 * k - 3 * (k // 2), 0)
        for h in range(2):
            for e in range(1, 4):
                part(h, e if h == 0 else d, d if h == 0 else e).wait_recv()
        for h in range(2):
            sources = [part_send[h, d if h == 0 else d * 4]]
            sources += [part_in[h, e * 4 + d if h == 0 else d * 4 + e] for e in range(1, 4)]
            mid_send[h, d] = encode([merged(sources, r) for r in range(2)])

        @pl.when(d > 0)
        def _():
            for h in range(2):
                last(h, d).start()

        return carry

    lax.fori_loop(0, 4, middle, 0)
    for h in range(2):
        for d in DIST:
            last(h, d).wait_recv()
    for r in range(2):
        pieces = []
        for h in range(2):
            value, level = fresh[r]
            sources = [mid_send[h, 0]] + [mid_in[h, d] for d in DIST]
            pieces.append(merged(sources, r, (value[32 * h:32 * h + 32], value[64 + 32 * h:96 + 32 * h], level)))
        soft_ref[r] = jnp.concatenate([pieces[0][0], pieces[1][0], pieces[0][1], pieces[1][1]], axis=0).T

    def finish(n, carry):
        half(0, 0, n, at_offset(1, 0)).wait_send()
        half(1, 0, n, at_offset(1, 0)).wait_send()
        lin = lin_back(n)
        lin.wait_recv()
        lin.wait_send()
        dz, dy = offsets(n)

        @pl.when(dz > 0)
        def _():
            part(0, dz, dy).wait_send()

        @pl.when(dy > 0)
        def _():
            part(1, dz, dy).wait_send()

        return carry

    lax.fori_loop(1, N, finish, 0)
    for copy in mids + lasts + [last(h, d) for h in range(2) for d in DIST]:
        copy.wait_send()

    def place(n, carry):
        dz, dy = offsets(n)
        rows = pl.ds(pl.multiple_of(at_offset(dz, dy) * 8, 8), 8)
        for r in range(2):
            lin_out[r, rows] = lin_in[n, r]
        return carry

    for r in range(2):
        lin_out[r, pl.ds(pl.multiple_of(me * 8, 8), 8)] = lin_send[0, r]
    lax.fori_loop(1, N, place, 0)
    for r in range(2):
        y = lin_fresh[2] * lin_out[r] + lin_fresh[r]
        lin_ref[r] = y / jnp.sqrt(jnp.mean(y * y, axis=1, keepdims=True) + 1e-5)


def copy_kernel(a_ref, b_ref, c_ref, d_ref):
    c_ref[...] = a_ref[...]
    d_ref[...] = b_ref[...]


def rows_first(x):
    return x.reshape(2, 2, 64, WIDTH).transpose(0, 2, 1, 3).reshape(2, WIDTH, WIDTH)


def pairs_first(x):
    return x.reshape(2, 2, 2, 64, WIDTH).transpose(0, 1, 3, 2, 4).reshape(2, 2, WIDTH, WIDTH)


def rows_last(x):
    return x.reshape(2, 64, 2, WIDTH).transpose(0, 2, 1, 3).reshape(2, 2, 64 * WIDTH)


def shards(
    request_owner, page_list, context_len, lin_state, decay_rate, lin_query, lin_keyval, soft_query, new_keyval,
    page_pool,
):
    vmem = pl.BlockSpec(memory_space=pltpu.VMEM)
    hbm = pl.BlockSpec(memory_space=pl.ANY)
    out = [jax.ShapeDtypeStruct((2, WIDTH, WIDTH), jnp.float32)] * 2
    lin, soft = pl.pallas_call(
        kernel,
        out_shape=out,
        in_specs=[vmem] * 4 + [hbm] * 6,
        out_specs=[vmem] * 2,
        scratch_shapes=[
            pltpu.VMEM(lin_state.shape, jnp.float32),
            pltpu.VMEM(page_pool.shape, jnp.bfloat16),
            pltpu.VMEM((2, WIDTH, WIDTH), jnp.bfloat16),
            pltpu.VMEM(new_keyval.shape, jnp.bfloat16),
            pltpu.VMEM((2, WIDTH, WIDTH), jnp.bfloat16),
            pltpu.VMEM((2, 2, WIDTH, WIDTH), jnp.bfloat16),
            pltpu.VMEM((3, WIDTH, WIDTH), jnp.float32),
            pltpu.VMEM((2, WIDTH, WIDTH), jnp.float32),
            pltpu.VMEM((N, 2, WIDTH, WIDTH), jnp.bfloat16),
            pltpu.VMEM((4, 4, 16, WIDTH), jnp.bfloat16),
            pltpu.VMEM((4, 4, 16, WIDTH), jnp.bfloat16),
            pltpu.VMEM((4, 4, 16, WIDTH), jnp.bfloat16),
            pltpu.VMEM((N, 2, 8, WIDTH), jnp.float32),
            pltpu.VMEM((N, 2, 8, WIDTH), jnp.float32),
            pltpu.VMEM((2, N, 72, WIDTH), jnp.int32),
            pltpu.VMEM((2, N, 72, WIDTH), jnp.int32),
            pltpu.VMEM((2, 4, 72, WIDTH), jnp.int32),
            pltpu.VMEM((2, 4, 72, WIDTH), jnp.int32),
            pltpu.VMEM((8, WIDTH), jnp.int32),
            pltpu.SMEM((8, WIDTH), jnp.int32),
            pltpu.SemaphoreType.DMA((9,)),
            pltpu.SemaphoreType.DMA((2, N)),
            pltpu.SemaphoreType.DMA((2, N)),
            pltpu.SemaphoreType.DMA((2, 4)),
            pltpu.SemaphoreType.DMA((2, 4)),
            pltpu.SemaphoreType.DMA((N,)),
            pltpu.SemaphoreType.DMA((N,)),
            pltpu.SemaphoreType.DMA((2, N)),
            pltpu.SemaphoreType.DMA((2, N)),
            pltpu.SemaphoreType.DMA((2, 4)),
            pltpu.SemaphoreType.DMA((2, 4)),
        ],
        compiler_params=pltpu.CompilerParams(
            collective_id=0, has_side_effects=True, vmem_limit_bytes=56 * 1024 * 1024
        ),
    )(
        request_owner.reshape(1, 32), page_list.T, context_len.reshape(1, 32), decay_rate.reshape(1, 64),
        rows_first(soft_query), new_keyval, rows_first(lin_query), pairs_first(lin_keyval), lin_state, page_pool,
    )
    lin, soft = pl.pallas_call(copy_kernel, out_shape=out, in_specs=[vmem] * 2, out_specs=[vmem] * 2)(lin, soft)
    return rows_last(lin), rows_last(soft)


def solution(mesh):
    return jax.shard_map(
        shards,
        mesh=mesh,
        in_specs=(
            P("grp"), P("grp", None), P("grp"), P("grp", "head", None, None), P(),
            P(("grp", "head"), None, None), P(("grp", "head"), None, None, None),
            P(("grp", "head"), None, None), P(("grp", "head"), None, None, None),
            P(("grp", "head"), None, None, None),
        ),
        out_specs=(P(("grp", "head"), None, None), P(("grp", "head"), None, None)),
        check_vma=False,
    )
```

```python
import functools
import math

import jax
import jax.numpy as jnp
from jax import lax
from jax.experimental import pallas as pl
from jax.experimental.pallas import tpu as pltpu
from jax.sharding import PartitionSpec as P

MESH = pl.DeviceIdType.MESH
N = 16
WIDTH = 128
KVH = 8
CODES = 32000.0
LOW = -1e30
NONE = -505.0
LEVEL_UNIT = 2.0**22
SIZE_UNIT = 2.0**16
SCALE = 1.0 / math.sqrt(128.0)


DIST = (1, 3, 2)
OFFSETS = ((0, 0), (1, 0), (0, 1), (3, 0), (0, 3), (2, 0), (0, 2), (1, 1), (1, 3), (3, 1), (1, 2), (2, 1), (3, 3), (3, 2), (2, 3), (2, 2))
SLOT = {offset: n for n, offset in enumerate(OFFSETS)}


def offsets(n):
    return tuple(
        sum(jnp.where(n == i, offset[axis], 0) for i, offset in enumerate(OFFSETS) if offset[axis]) for axis in (0, 1)
    )


def make_tables(owner, pages, length, me):
    sub = lax.broadcasted_iota(jnp.int32, (32, 32), 0)
    lane = lax.broadcasted_iota(jnp.int32, (32, 32), 1)

    def column(row):
        return jnp.sum(jnp.where(sub == lane, row, 0), axis=1, keepdims=True)

    slot = jnp.sum(jnp.where((column(owner) == owner) & (sub < lane), 1, 0), axis=0, keepdims=True)
    row = owner * 2 + slot
    request_of = jnp.sum(jnp.where(column(row) == lane, sub, 0), axis=0, keepdims=True)
    j = lax.broadcasted_iota(jnp.int32, (8, 32), 0)
    count = jnp.clip(length - j * WIDTH, 0, WIDTH)
    here = (lax.shift_right_logical(pages, 4) == me) & (count > 0)
    code = (pages & 15) + count * 16
    least = jnp.min(jnp.where(here, j, 8), axis=0, keepdims=True)
    most = jnp.max(jnp.where(here, j, -1), axis=0, keepdims=True)
    first = jnp.sum(jnp.where(here & (j == least), code, 0), axis=0, keepdims=True)
    second = jnp.sum(jnp.where(here & (j == most) & (most != least), code, 0), axis=0, keepdims=True)
    return request_of, first, second


def kernel(
    owner, pages, length, rate, sq_hbm, nkv_hbm, lq_hbm, lkv_hbm, state_hbm, pool_hbm, lin_ref, soft_ref,
    state, pool, sq, nkv, lq, lkv, lin_fresh, lin_out, fresh, fresh_log, q_all, lin_pack, lin_mid, lin_all, lin_send, lin_in, part_send, part_in, mid_send, mid_in,
    tab_rows, tab, local_sem, half_send, half_recv, mid_sems, mid_recvs, back_send, back_recv,
    part_sems, part_recvs, last_sems, last_recvs,
):
    me = lax.axis_index("head")
    mz, my = me // 4, me % 4

    def at_offset(dz, dy):
        return (mz + dz) % 4 * 4 + (my + dy) % 4

    def behind(n):
        dz, dy = offsets(n)
        return at_offset(4 - dz, 4 - dy)

    def remote(src, dst, send, recv, to):
        return pltpu.make_async_remote_copy(
            src_ref=src, dst_ref=dst, send_sem=send, recv_sem=recv, device_id={"head": to}, device_id_type=MESH
        )

    def half(h, src, dst, to):
        rows = pl.ds(64 * h, 64)
        return remote(
            q_all.at[src, :, rows], q_all.at[dst, :, rows], half_send.at[h, dst], half_recv.at[h, dst], to
        )

    def lin_back(n):
        return remote(lin_send.at[n], lin_in.at[n], back_send.at[n], back_recv.at[n], behind(n))

    def part(h, dz, dy):
        to = at_offset(4 - dz, 0) if h == 0 else at_offset(0, 4 - dy)
        n = dz * 4 + dy
        return remote(part_send.at[h, n], part_in.at[h, n], part_sems.at[h, n], part_recvs.at[h, n], to)

    def last(h, d):
        to = at_offset(0, 4 - d) if h == 0 else at_offset(4 - d, 0)
        return remote(mid_send.at[h, d], mid_in.at[h, d], last_sems.at[h, d], last_recvs.at[h, d], to)

    barrier = pltpu.get_barrier_semaphore()
    for d in DIST:
        for to in (at_offset(d, 0), at_offset(0, d)):
            pl.semaphore_signal(barrier, inc=1, device_id={"head": to}, device_id_type=MESH)
    loads = [
        pltpu.make_async_copy(src, dst, local_sem.at[5 + n])
        for n, (src, dst) in enumerate(((sq_hbm, sq), (lq_hbm, lq), (lkv_hbm, lkv), (nkv_hbm, nkv)))
    ]
    for copy in loads:
        copy.start()
    fetch_pool = pltpu.make_async_copy(pool_hbm, pool, local_sem.at[1])
    fetch_state = pltpu.make_async_copy(state_hbm, state, local_sem.at[0])
    fetch_pool.start()
    fetch_state.start()
    tab_rows[...] = jnp.zeros((8, WIDTH), jnp.int32)
    for n, row in enumerate(make_tables(owner[...], pages[...], length[...], me)):
        tab_rows[n:n + 1, 0:32] = row
    fill_tab = pltpu.make_async_copy(tab_rows, tab, local_sem.at[4])
    fill_tab.start()
    for copy in loads:
        copy.wait()
    wide = [lq[r].astype(jnp.float32) for r in range(2)]
    for peer in range(N):
        lin_pack[peer // 4, peer % 4] = jnp.concatenate(
            [x[peer * 8:peer * 8 + 8] for x in wide], axis=0
        ).astype(jnp.bfloat16)
    own_mid = pltpu.make_async_copy(lin_pack.at[mz], lin_mid.at[0], local_sem.at[2])
    own_mid.start()
    for r in range(2):
        q_all[0, r] = sq[r].astype(jnp.float32).T.astype(jnp.bfloat16)

    row_of = lax.broadcasted_iota(jnp.int32, (WIDTH, 64), 0)
    lane_of = lax.broadcasted_iota(jnp.int32, (WIDTH, 64), 1)
    rates = jnp.sum(jnp.where(lane_of == row_of // 2, rate[...], 0.0), axis=1, keepdims=True)
    second = lax.broadcasted_iota(jnp.int32, (WIDTH, 1), 0) % 2 == 1
    lam = jnp.exp(-rates)
    lam_state = jnp.where(second, lam * lam, lam)
    lam_first = jnp.where(second, lam, 1.0)
    lam_second = jnp.where(second, 1.0, 0.0)
    odd = lax.broadcasted_iota(jnp.int32, (WIDTH, WIDTH), 0) % 2 == 1

    def keys_values(x):
        return jnp.where(odd, pltpu.roll(x, 1, 0), x), jnp.where(odd, x, pltpu.roll(x, WIDTH - 1, 0))

    for r in range(2):
        k1, v1 = keys_values(lkv[r, 0].astype(jnp.float32))
        k2, v2 = keys_values(lkv[r, 1].astype(jnp.float32))
        qk1 = jnp.sum(wide[r] * k1, axis=1, keepdims=True)
        qk2 = jnp.sum(wide[r] * k2, axis=1, keepdims=True)
        lin_fresh[r] = (lam_first * qk1) * v1 + (lam_second * qk2) * v2
    lin_fresh[2] = jnp.broadcast_to(lam_state, (WIDTH, WIDTH))
    step = lax.broadcasted_iota(jnp.int32, (1, WIDTH), 1) % 2

    def by_head(x):
        return jnp.concatenate(
            [jnp.broadcast_to(x[:, c * WIDTH:(c + 1) * WIDTH], (16, WIDTH)) for c in range(KVH)], axis=0
        ).T

    for r in range(2):
        q = q_all[0, r].astype(jnp.float32)
        kv = [nkv[r, t].astype(jnp.float32) for t in range(2)]
        s0 = jnp.sum(q * by_head(kv[0][0:1]), axis=0, keepdims=True) * SCALE
        s1 = jnp.sum(q * by_head(kv[1][0:1]), axis=0, keepdims=True) * SCALE
        top = jnp.where(step == 1, jnp.maximum(s0, s1), s0)
        w0 = jnp.exp(s0 - top)
        w1 = jnp.where(step == 1, jnp.exp(s1 - top), 0.0)
        r0 = w0.astype(jnp.bfloat16).astype(jnp.float32)
        r1 = w1.astype(jnp.bfloat16).astype(jnp.float32)
        fresh[r] = (r0 * by_head(kv[0][1:2]) + r1 * by_head(kv[1][1:2])) / (w0 + w1)
        fresh_log[r:r + 1] = top + jnp.log(w0 + w1)
    pl.semaphore_wait(barrier, 6)

    mids = [
        remote(lin_pack.at[(mz + d) % 4], lin_mid.at[d], mid_sems.at[0, d], mid_recvs.at[0, d], at_offset(d, 0))
        for d in DIST
    ]
    for copy in mids:
        copy.start()

    first = {}
    for d in DIST:
        first[0, d] = half(0, 0, SLOT[d, 0], at_offset(d, 0))
        first[1, d] = half(1, 0, SLOT[0, d], at_offset(0, d))
    for copy in first.values():
        copy.start()
    for d in DIST:
        half(0, 0, SLOT[0, d], at_offset(0, d)).start()
        half(1, 0, SLOT[d, 0], at_offset(d, 0)).start()
    own_mid.wait()
    for copy in mids:
        copy.wait_recv()
    lasts = [
        remote(
            lin_mid.at[:, (my + d) % 4], lin_all.at[d], mid_sems.at[1, d], mid_recvs.at[1, d], at_offset(0, d)
        )
        for d in DIST
    ]
    for copy in lasts:
        copy.start()
    own_last = pltpu.make_async_copy(lin_mid.at[:, my], lin_all.at[0], local_sem.at[3])
    own_last.start()
    here = set()
    for dz, dy in OFFSETS[7:]:
        for h, d in ((0, dz), (1, dy)):
            if (h, d) not in here:
                first[h, d].wait_recv()
                here.add((h, d))
        half(0, SLOT[dz, 0], SLOT[dz, dy], at_offset(0, dy)).start()
        half(1, SLOT[0, dy], SLOT[dz, dy], at_offset(dz, 0)).start()

    head_of = lax.broadcasted_iota(jnp.int32, (8, WIDTH), 0) // 2

    def lightning(n):
        dz, dy = offsets(n)
        owner_at = behind(n)
        block = lin_all[dy, dz].astype(jnp.float32)
        for r in range(2):
            request = tab[0, owner_at * 2 + r] & 31
            q = block[8 * r:8 * r + 8].astype(jnp.bfloat16)
            q_two = jnp.concatenate([q, q], axis=1)
            y = jnp.zeros((8, WIDTH), jnp.float32)
            for h in range(4):
                s = state[request, h]
                high = s.astype(jnp.bfloat16)
                low = (s - high.astype(jnp.float32)).astype(jnp.bfloat16)
                got = jnp.dot(q_two, jnp.concatenate([high, low], axis=0), preferred_element_type=jnp.float32)
                y = jnp.where(head_of == h, got, y)
            lin_send[n, r] = y

    position = lax.broadcasted_iota(jnp.int32, (WIDTH, WIDTH), 0)
    lane_head = lax.broadcasted_iota(jnp.int32, (WIDTH, WIDTH), 1) // 16
    of_head = [jnp.where(lane_head == c, 1.0, 0.0).astype(jnp.bfloat16) for c in range(KVH)]

    def page_part(page, count, q):
        scores = sum(
            jnp.dot(
                pool[page, 0, :, c * WIDTH:(c + 1) * WIDTH], q * of_head[c], preferred_element_type=jnp.float32
            )
            for c in range(KVH)
        ) * SCALE
        live = position < count
        top = jnp.max(jnp.where(live, scores, LOW), axis=0, keepdims=True)
        weight = jnp.where(live, jnp.exp(scores - top), 0.0)
        total = jnp.sum(weight, axis=0, keepdims=True)
        rounded = weight.astype(jnp.bfloat16)
        acc = sum(
            lax.dot_general(
                pool[page, 1, :, c * WIDTH:(c + 1) * WIDTH], rounded * of_head[c], (((0,), (0,)), ((), ())),
                preferred_element_type=jnp.float32,
            )
            for c in range(KVH)
        )
        return top, total, acc

    def encode(found):
        words, logs = [], []
        for upper, lower, level in found:
            most = jnp.maximum(
                jnp.max(jnp.abs(upper), axis=0, keepdims=True), jnp.max(jnp.abs(lower), axis=0, keepdims=True)
            )
            size = jnp.ceil(jnp.log(jnp.maximum(most, 1e-30)) * SIZE_UNIT)
            inverse = CODES * jnp.exp(size * (-1.0 / SIZE_UNIT))
            high = (upper * inverse + 32768.5).astype(jnp.int32)
            low = (lower * inverse + 32768.5).astype(jnp.int32)
            words.append(lax.shift_left(high, 16) | low)
            logs += [(level * LEVEL_UNIT).astype(jnp.int32), size.astype(jnp.int32)]
        return jnp.concatenate(words + logs, axis=0)

    def merged(sources, r, more=None):
        levels = [x[64 + 2 * r:65 + 2 * r].astype(jnp.float32) * (1.0 / LEVEL_UNIT) for x in sources]
        sizes = [x[65 + 2 * r:66 + 2 * r].astype(jnp.float32) * (1.0 / SIZE_UNIT) for x in sources]
        peak = functools.reduce(jnp.maximum, levels + ([more[2]] if more else []))
        weights = [jnp.where(x > NONE + 20.0, jnp.exp(x - peak), 0.0) for x in levels]
        total = sum(weights)
        factors = [w * jnp.exp(size) * (1.0 / CODES) for w, size in zip(weights, sizes)]
        shift = sum(factors) * 32768.0
        upper, lower = -shift, -shift
        if more:
            weight = jnp.exp(more[2] - peak)
            total = total + weight
            upper, lower = weight * more[0] - shift, weight * more[1] - shift
        for factor, x in zip(factors, sources):
            words = x[32 * r:32 * r + 32]
            upper = upper + factor * lax.shift_right_logical(words, 16).astype(jnp.float32)
            lower = lower + factor * (words & 65535).astype(jnp.float32)
        total = jnp.maximum(total, 1e-30)
        inverse = 1.0 / total
        return upper * inverse, lower * inverse, jnp.maximum(peak + jnp.log(total), NONE)

    def softmax(n):
        dz, dy = offsets(n)
        owner_at = behind(n)
        a, b = tab[0, owner_at * 2] & 31, tab[0, owner_at * 2 + 1] & 31
        first_a, second_a, first_b, second_b = tab[1, a], tab[2, a], tab[1, b], tab[2, b]
        codes = (
            jnp.where(first_a > 0, first_a, first_b),
            jnp.where(second_a > 0, second_a, jnp.where(first_a > 0, first_b, second_b)),
        )
        rows = (jnp.where(first_a > 0, 0, 1), jnp.where(second_a > 0, 0, 1))
        found = []
        for code, row in zip(codes, rows):
            q = jnp.where(row == 1, q_all[n, 1], q_all[n, 0])
            found.append((row, *page_part(code & 15, lax.shift_right_logical(code, 4), q)))
        values = []
        for r in range(2):
            tops = [jnp.where(row == r, top, LOW) for row, top, _, _ in found]
            peak = jnp.maximum(tops[0], tops[1])
            factors = [jnp.where(row == r, jnp.exp(t - peak), 0.0) for t, (row, _, _, _) in zip(tops, found)]
            total = jnp.maximum(factors[0] * found[0][2] + factors[1] * found[1][2], 1e-30)
            inverse = 1.0 / total
            value = (factors[0] * inverse) * found[0][3] + (factors[1] * inverse) * found[1][3]
            values.append((value, jnp.maximum(peak + jnp.log(total), NONE)))
        for h in range(2):
            part_send[h, dz * 4 + dy] = encode(
                [(v[32 * h:32 * h + 32], v[64 + 32 * h:96 + 32 * h], level) for v, level in values]
            )

    fetch_pool.wait()
    fill_tab.wait()

    def lightning_pair(p, carry):
        for n in (2 * p, 2 * p + 1):
            lightning(n)
        for n in (2 * p, 2 * p + 1):

            @pl.when(n > 0)
            def _(n=n):
                lin_back(n).start()

        return carry

    def pair(p, carry):
        for n in (2 * p, 2 * p + 1):
            dz, dy = offsets(n)

            @pl.when(dy > 0)
            def _(n=n):
                half(0, 0, n, at_offset(1, 0)).wait_recv()

            @pl.when(dz > 0)
            def _(n=n):
                half(1, 0, n, at_offset(1, 0)).wait_recv()

        for n in (2 * p, 2 * p + 1):
            softmax(n)
        for n in (2 * p, 2 * p + 1):
            dz, dy = offsets(n)

            @pl.when(dz > 0)
            def _(dz=dz, dy=dy):
                part(0, dz, dy).start()

            @pl.when(dy > 0)
            def _(dz=dz, dy=dy):
                part(1, dz, dy).start()

        return carry

    lax.fori_loop(0, 8, pair, 0)
    own_last.wait()
    for copy in lasts:
        copy.wait_recv()
    fetch_state.wait()
    lax.fori_loop(0, 8, lightning_pair, 0)

    def middle(k, carry):
        d = jnp.where(k < 3, 1 + 2 * k - 3 * (k // 2), 0)
        for h in range(2):
            for e in range(1, 4):
                part(h, e if h == 0 else d, d if h == 0 else e).wait_recv()
        for h in range(2):
            sources = [part_send[h, d if h == 0 else d * 4]]
            sources += [part_in[h, e * 4 + d if h == 0 else d * 4 + e] for e in range(1, 4)]
            mid_send[h, d] = encode([merged(sources, r) for r in range(2)])

        @pl.when(d > 0)
        def _():
            for h in range(2):
                last(h, d).start()

        return carry

    lax.fori_loop(0, 4, middle, 0)

    def place(n, carry):
        lin_back(n).wait_recv()
        dz, dy = offsets(n)
        rows = pl.ds(pl.multiple_of(at_offset(dz, dy) * 8, 8), 8)
        for r in range(2):
            lin_out[r, rows] = lin_in[n, r]
        return carry

    for r in range(2):
        lin_out[r, pl.ds(pl.multiple_of(me * 8, 8), 8)] = lin_send[0, r]
    lax.fori_loop(1, N, place, 0)
    for r in range(2):
        y = lin_fresh[2] * lin_out[r] + lin_fresh[r]
        lin_ref[r] = y / jnp.sqrt(jnp.mean(y * y, axis=1, keepdims=True) + 1e-5)

    for h in range(2):
        for d in DIST:
            last(h, d).wait_recv()
    for r in range(2):
        pieces = []
        for h in range(2):
            value, level = fresh[r], fresh_log[r:r + 1]
            sources = [mid_send[h, 0]] + [mid_in[h, d] for d in DIST]
            pieces.append(merged(sources, r, (value[32 * h:32 * h + 32], value[64 + 32 * h:96 + 32 * h], level)))
        soft_ref[r] = jnp.concatenate([pieces[0][0], pieces[1][0], pieces[0][1], pieces[1][1]], axis=0).T

    def finish(n, carry):
        half(0, 0, n, at_offset(1, 0)).wait_send()
        half(1, 0, n, at_offset(1, 0)).wait_send()
        lin_back(n).wait_send()
        dz, dy = offsets(n)

        @pl.when(dz > 0)
        def _():
            part(0, dz, dy).wait_send()

        @pl.when(dy > 0)
        def _():
            part(1, dz, dy).wait_send()

        return carry

    lax.fori_loop(1, N, finish, 0)
    for copy in mids + lasts + [last(h, d) for h in range(2) for d in DIST]:
        copy.wait_send()


def copy_kernel(a_ref, b_ref, c_ref, d_ref):
    c_ref[...] = a_ref[...]
    d_ref[...] = b_ref[...]


def rows_first(x):
    return x.reshape(2, 2, 64, WIDTH).transpose(0, 2, 1, 3).reshape(2, WIDTH, WIDTH)


def pairs_first(x):
    return x.reshape(2, 2, 2, 64, WIDTH).transpose(0, 1, 3, 2, 4).reshape(2, 2, WIDTH, WIDTH)


def rows_last(x):
    return x.reshape(2, 64, 2, WIDTH).transpose(0, 2, 1, 3).reshape(2, 2, 64 * WIDTH)


def shards(
    request_owner, page_list, context_len, lin_state, decay_rate, lin_query, lin_keyval, soft_query, new_keyval,
    page_pool,
):
    vmem = pl.BlockSpec(memory_space=pltpu.VMEM)
    hbm = pl.BlockSpec(memory_space=pl.ANY)
    out = [jax.ShapeDtypeStruct((2, WIDTH, WIDTH), jnp.float32)] * 2
    lin, soft = pl.pallas_call(
        kernel,
        out_shape=[pltpu.VMEM((2, WIDTH, WIDTH), jnp.float32)] * 2,
        in_specs=[vmem] * 4 + [hbm] * 6,
        out_specs=[vmem] * 2,
        scratch_shapes=[
            pltpu.VMEM(lin_state.shape, jnp.float32),
            pltpu.VMEM(page_pool.shape, jnp.bfloat16),
            pltpu.VMEM((2, WIDTH, WIDTH), jnp.bfloat16),
            pltpu.VMEM(new_keyval.shape, jnp.bfloat16),
            pltpu.VMEM((2, WIDTH, WIDTH), jnp.bfloat16),
            pltpu.VMEM((2, 2, WIDTH, WIDTH), jnp.bfloat16),
            pltpu.VMEM((3, WIDTH, WIDTH), jnp.float32),
            pltpu.VMEM((2, WIDTH, WIDTH), jnp.float32),
            pltpu.VMEM((2, WIDTH, WIDTH), jnp.float32),
            pltpu.VMEM((8, WIDTH), jnp.float32),
            pltpu.VMEM((N, 2, WIDTH, WIDTH), jnp.bfloat16),
            pltpu.VMEM((4, 4, 16, WIDTH), jnp.bfloat16),
            pltpu.VMEM((4, 4, 16, WIDTH), jnp.bfloat16),
            pltpu.VMEM((4, 4, 16, WIDTH), jnp.bfloat16),
            pltpu.VMEM((N, 2, 8, WIDTH), jnp.float32),
            pltpu.VMEM((N, 2, 8, WIDTH), jnp.float32),
            pltpu.VMEM((2, N, 68, WIDTH), jnp.int32),
            pltpu.VMEM((2, N, 68, WIDTH), jnp.int32),
            pltpu.VMEM((2, 4, 68, WIDTH), jnp.int32),
            pltpu.VMEM((2, 4, 68, WIDTH), jnp.int32),
            pltpu.VMEM((8, WIDTH), jnp.int32),
            pltpu.SMEM((8, WIDTH), jnp.int32),
            pltpu.SemaphoreType.DMA((9,)),
            pltpu.SemaphoreType.DMA((2, N)),
            pltpu.SemaphoreType.DMA((2, N)),
            pltpu.SemaphoreType.DMA((2, 4)),
            pltpu.SemaphoreType.DMA((2, 4)),
            pltpu.SemaphoreType.DMA((N,)),
            pltpu.SemaphoreType.DMA((N,)),
            pltpu.SemaphoreType.DMA((2, N)),
            pltpu.SemaphoreType.DMA((2, N)),
            pltpu.SemaphoreType.DMA((2, 4)),
            pltpu.SemaphoreType.DMA((2, 4)),
        ],
        compiler_params=pltpu.CompilerParams(
            collective_id=0, has_side_effects=True, vmem_limit_bytes=56 * 1024 * 1024
        ),
    )(
        request_owner.reshape(1, 32), page_list.T, context_len.reshape(1, 32), decay_rate.reshape(1, 64),
        rows_first(soft_query), new_keyval, rows_first(lin_query), pairs_first(lin_keyval), lin_state, page_pool,
    )
    lin, soft = (pltpu.with_memory_space_constraint(x, pltpu.VMEM) for x in (lin, soft))
    lin, soft = pl.pallas_call(copy_kernel, out_shape=out, in_specs=[vmem] * 2, out_specs=[vmem] * 2)(lin, soft)
    return rows_last(lin), rows_last(soft)


def solution(mesh):
    return jax.shard_map(
        shards,
        mesh=mesh,
        in_specs=(
            P("grp"), P("grp", None), P("grp"), P("grp", "head", None, None), P(),
            P(("grp", "head"), None, None), P(("grp", "head"), None, None, None),
            P(("grp", "head"), None, None), P(("grp", "head"), None, None, None),
            P(("grp", "head"), None, None, None),
        ),
        out_specs=(P(("grp", "head"), None, None), P(("grp", "head"), None, None)),
        check_vma=False,
    )
```

```python
import functools
import math

import jax
import jax.numpy as jnp
from jax import lax
from jax.experimental import pallas as pl
from jax.experimental.pallas import tpu as pltpu
from jax.sharding import PartitionSpec as P

MESH = pl.DeviceIdType.MESH
N = 16
WIDTH = 128
KVH = 8
CODES = 32000.0
LOW = -1e30
NONE = -505.0
LEVEL_UNIT = 2.0**22
SIZE_UNIT = 2.0**16
SCALE = 1.0 / math.sqrt(128.0)


DIST = (1, 3, 2)
OFFSETS = ((0, 0), (1, 0), (0, 1), (3, 0), (0, 3), (2, 0), (0, 2), (1, 1), (1, 3), (3, 1), (1, 2), (2, 1), (3, 3), (3, 2), (2, 3), (2, 2))
SLOT = {offset: n for n, offset in enumerate(OFFSETS)}


def packed(axis):
    bits = sum(offset[axis] << 2 * n for n, offset in enumerate(OFFSETS))
    return bits - (1 << 32) if bits >= 1 << 31 else bits


def offsets(n):
    return tuple(lax.shift_right_logical(jnp.int32(packed(axis)), jnp.int32(2 * n)) & 3 for axis in (0, 1))


def make_tables(owner, pages, length, me):
    sub = lax.broadcasted_iota(jnp.int32, (32, 32), 0)
    lane = lax.broadcasted_iota(jnp.int32, (32, 32), 1)

    def column(row):
        return jnp.sum(jnp.where(sub == lane, row, 0), axis=1, keepdims=True)

    slot = jnp.sum(jnp.where((column(owner) == owner) & (sub < lane), 1, 0), axis=0, keepdims=True)
    row = owner * 2 + slot
    request_of = jnp.sum(jnp.where(column(row) == lane, sub, 0), axis=0, keepdims=True)
    j = lax.broadcasted_iota(jnp.int32, (8, 32), 0)
    count = jnp.clip(length - j * WIDTH, 0, WIDTH)
    here = (lax.shift_right_logical(pages, 4) == me) & (count > 0)
    code = (pages & 15) + count * 16
    least = jnp.min(jnp.where(here, j, 8), axis=0, keepdims=True)
    most = jnp.max(jnp.where(here, j, -1), axis=0, keepdims=True)
    first = jnp.sum(jnp.where(here & (j == least), code, 0), axis=0, keepdims=True)
    second = jnp.sum(jnp.where(here & (j == most) & (most != least), code, 0), axis=0, keepdims=True)
    return request_of, first, second


def kernel(
    owner_hbm, pages_hbm, length_hbm, rate_hbm, sq_hbm, nkv_hbm, lq_hbm, lkv_hbm, state_hbm, pool_hbm, lin_ref, soft_ref,
    state, pool, owner, pages, length, rate, sq, nkv, lq, lkv, lin_fresh, lin_out, fresh, fresh_log, q_all, lin_pack, lin_mid, lin_all, lin_send, lin_in, part_send, part_in, mid_send, mid_in,
    tab_rows, tab, local_sem, half_send, half_recv, mid_sems, mid_recvs, back_send, back_recv,
    part_sems, part_recvs, last_sems, last_recvs,
):
    me = lax.axis_index("head")
    mz, my = me // 4, me % 4

    def at_offset(dz, dy):
        return (mz + dz) % 4 * 4 + (my + dy) % 4

    def behind(n):
        dz, dy = offsets(n)
        return at_offset(4 - dz, 4 - dy)

    def remote(src, dst, send, recv, to):
        return pltpu.make_async_remote_copy(
            src_ref=src, dst_ref=dst, send_sem=send, recv_sem=recv, device_id={"head": to}, device_id_type=MESH
        )

    def half(h, src, dst, to):
        rows = pl.ds(64 * h, 64)
        return remote(
            q_all.at[src, :, rows], q_all.at[dst, :, rows], half_send.at[h, dst], half_recv.at[h, dst], to
        )

    def lin_back(n):
        return remote(lin_send.at[n], lin_in.at[n], back_send.at[n], back_recv.at[n], behind(n))

    def part(h, dz, dy):
        to = at_offset(4 - dz, 0) if h == 0 else at_offset(0, 4 - dy)
        n = dz * 4 + dy
        return remote(part_send.at[h, n], part_in.at[h, n], part_sems.at[h, n], part_recvs.at[h, n], to)

    def last(h, d):
        to = at_offset(0, 4 - d) if h == 0 else at_offset(4 - d, 0)
        return remote(mid_send.at[h, d], mid_in.at[h, d], last_sems.at[h, d], last_recvs.at[h, d], to)

    barrier = pltpu.get_barrier_semaphore()
    for d in DIST:
        for to in (at_offset(d, 0), at_offset(0, d)):
            pl.semaphore_signal(barrier, inc=1, device_id={"head": to}, device_id_type=MESH)
    loads = [
        pltpu.make_async_copy(src, dst, local_sem.at[5 + n])
        for n, (src, dst) in enumerate(
            (
                (owner_hbm, owner), (pages_hbm, pages), (length_hbm, length), (rate_hbm, rate),
                (sq_hbm, sq), (lq_hbm, lq), (lkv_hbm, lkv), (nkv_hbm, nkv),
            )
        )
    ]
    for copy in loads:
        copy.start()
    fetch_pool = pltpu.make_async_copy(pool_hbm, pool, local_sem.at[1])
    fetch_state = pltpu.make_async_copy(state_hbm, state, local_sem.at[0])
    fetch_pool.start()
    fetch_state.start()
    for copy in loads:
        copy.wait()
    tab_rows[...] = jnp.zeros((8, WIDTH), jnp.int32)
    for n, row in enumerate(make_tables(owner[...], pages[...], length[...], me)):
        tab_rows[n:n + 1, 0:32] = row
    fill_tab = pltpu.make_async_copy(tab_rows, tab, local_sem.at[4])
    fill_tab.start()
    wide = [lq[r].astype(jnp.float32) for r in range(2)]
    for peer in range(N):
        lin_pack[peer // 4, peer % 4] = jnp.concatenate(
            [x[peer * 8:peer * 8 + 8] for x in wide], axis=0
        ).astype(jnp.bfloat16)
    own_mid = pltpu.make_async_copy(lin_pack.at[mz], lin_mid.at[0], local_sem.at[2])
    own_mid.start()
    for r in range(2):
        q_all[0, r] = sq[r].astype(jnp.float32).T.astype(jnp.bfloat16)

    row_of = lax.broadcasted_iota(jnp.int32, (WIDTH, 64), 0)
    lane_of = lax.broadcasted_iota(jnp.int32, (WIDTH, 64), 1)
    rates = jnp.sum(jnp.where(lane_of == row_of // 2, rate[...], 0.0), axis=1, keepdims=True)
    second = lax.broadcasted_iota(jnp.int32, (WIDTH, 1), 0) % 2 == 1
    lam = jnp.exp(-rates)
    lam_state = jnp.where(second, lam * lam, lam)
    lam_first = jnp.where(second, lam, 1.0)
    lam_second = jnp.where(second, 1.0, 0.0)
    odd = lax.broadcasted_iota(jnp.int32, (WIDTH, WIDTH), 0) % 2 == 1

    def keys_values(x):
        return jnp.where(odd, pltpu.roll(x, 1, 0), x), jnp.where(odd, x, pltpu.roll(x, WIDTH - 1, 0))

    for r in range(2):
        k1, v1 = keys_values(lkv[r, 0].astype(jnp.float32))
        k2, v2 = keys_values(lkv[r, 1].astype(jnp.float32))
        qk1 = jnp.sum(wide[r] * k1, axis=1, keepdims=True)
        qk2 = jnp.sum(wide[r] * k2, axis=1, keepdims=True)
        lin_fresh[r] = (lam_first * qk1) * v1 + (lam_second * qk2) * v2
    lin_fresh[2] = jnp.broadcast_to(lam_state, (WIDTH, WIDTH))
    step = lax.broadcasted_iota(jnp.int32, (1, WIDTH), 1) % 2

    def by_head(x):
        return jnp.concatenate(
            [jnp.broadcast_to(x[:, c * WIDTH:(c + 1) * WIDTH], (16, WIDTH)) for c in range(KVH)], axis=0
        ).T

    for r in range(2):
        q = q_all[0, r].astype(jnp.float32)
        kv = [nkv[r, t].astype(jnp.float32) for t in range(2)]
        s0 = jnp.sum(q * by_head(kv[0][0:1]), axis=0, keepdims=True) * SCALE
        s1 = jnp.sum(q * by_head(kv[1][0:1]), axis=0, keepdims=True) * SCALE
        top = jnp.where(step == 1, jnp.maximum(s0, s1), s0)
        w0 = jnp.exp(s0 - top)
        w1 = jnp.where(step == 1, jnp.exp(s1 - top), 0.0)
        r0 = w0.astype(jnp.bfloat16).astype(jnp.float32)
        r1 = w1.astype(jnp.bfloat16).astype(jnp.float32)
        fresh[r] = (r0 * by_head(kv[0][1:2]) + r1 * by_head(kv[1][1:2])) / (w0 + w1)
        fresh_log[r:r + 1] = top + jnp.log(w0 + w1)
    pl.semaphore_wait(barrier, 6)

    mids = [
        remote(lin_pack.at[(mz + d) % 4], lin_mid.at[d], mid_sems.at[0, d], mid_recvs.at[0, d], at_offset(d, 0))
        for d in DIST
    ]
    for copy in mids:
        copy.start()

    first = {}
    for d in DIST:
        first[0, d] = half(0, 0, SLOT[d, 0], at_offset(d, 0))
        first[1, d] = half(1, 0, SLOT[0, d], at_offset(0, d))
    for copy in first.values():
        copy.start()
    for d in DIST:
        half(0, 0, SLOT[0, d], at_offset(0, d)).start()
        half(1, 0, SLOT[d, 0], at_offset(d, 0)).start()
    own_mid.wait()
    for copy in mids:
        copy.wait_recv()
    lasts = [
        remote(
            lin_mid.at[:, (my + d) % 4], lin_all.at[d], mid_sems.at[1, d], mid_recvs.at[1, d], at_offset(0, d)
        )
        for d in DIST
    ]
    for copy in lasts:
        copy.start()
    own_last = pltpu.make_async_copy(lin_mid.at[:, my], lin_all.at[0], local_sem.at[3])
    own_last.start()
    here = set()
    for dz, dy in OFFSETS[7:]:
        for h, d in ((0, dz), (1, dy)):
            if (h, d) not in here:
                first[h, d].wait_recv()
                here.add((h, d))
        half(0, SLOT[dz, 0], SLOT[dz, dy], at_offset(0, dy)).start()
        half(1, SLOT[0, dy], SLOT[dz, dy], at_offset(dz, 0)).start()

    head_of = lax.broadcasted_iota(jnp.int32, (8, WIDTH), 0) // 2

    def lightning(n):
        dz, dy = offsets(n)
        owner_at = behind(n)
        block = lin_all[dy, dz].astype(jnp.float32)
        for r in range(2):
            request = tab[0, owner_at * 2 + r] & 31
            q = block[8 * r:8 * r + 8].astype(jnp.bfloat16)
            q_two = jnp.concatenate([q, q], axis=1)
            y = jnp.zeros((8, WIDTH), jnp.float32)
            for h in range(4):
                s = state[request, h]
                high = s.astype(jnp.bfloat16)
                low = (s - high.astype(jnp.float32)).astype(jnp.bfloat16)
                got = jnp.dot(q_two, jnp.concatenate([high, low], axis=0), preferred_element_type=jnp.float32)
                y = jnp.where(head_of == h, got, y)
            lin_send[n, r] = y

    position = lax.broadcasted_iota(jnp.int32, (WIDTH, WIDTH), 0)
    lane_head = lax.broadcasted_iota(jnp.int32, (WIDTH, WIDTH), 1) // 16
    of_head = [jnp.where(lane_head == c, 1.0, 0.0).astype(jnp.bfloat16) for c in range(KVH)]

    def page_part(page, count, q):
        scores = sum(
            jnp.dot(
                pool[page, 0, :, c * WIDTH:(c + 1) * WIDTH], q * of_head[c], preferred_element_type=jnp.float32
            )
            for c in range(KVH)
        ) * SCALE
        live = position < count
        top = jnp.max(jnp.where(live, scores, LOW), axis=0, keepdims=True)
        weight = jnp.where(live, jnp.exp(scores - top), 0.0)
        total = jnp.sum(weight, axis=0, keepdims=True)
        rounded = weight.astype(jnp.bfloat16)
        acc = sum(
            lax.dot_general(
                pool[page, 1, :, c * WIDTH:(c + 1) * WIDTH], rounded * of_head[c], (((0,), (0,)), ((), ())),
                preferred_element_type=jnp.float32,
            )
            for c in range(KVH)
        )
        return top, total, acc

    def encode(found):
        words, logs = [], []
        for upper, lower, level in found:
            most = jnp.maximum(
                jnp.max(jnp.abs(upper), axis=0, keepdims=True), jnp.max(jnp.abs(lower), axis=0, keepdims=True)
            )
            size = jnp.ceil(jnp.log(jnp.maximum(most, 1e-30)) * SIZE_UNIT)
            inverse = CODES * jnp.exp(size * (-1.0 / SIZE_UNIT))
            high = (upper * inverse + 32768.5).astype(jnp.int32)
            low = (lower * inverse + 32768.5).astype(jnp.int32)
            words.append(lax.shift_left(high, 16) | low)
            logs += [(level * LEVEL_UNIT).astype(jnp.int32), size.astype(jnp.int32)]
        return jnp.concatenate(words + logs, axis=0)

    def merged(sources, r, more=None):
        levels = [x[64 + 2 * r:65 + 2 * r].astype(jnp.float32) * (1.0 / LEVEL_UNIT) for x in sources]
        sizes = [x[65 + 2 * r:66 + 2 * r].astype(jnp.float32) * (1.0 / SIZE_UNIT) for x in sources]
        peak = functools.reduce(jnp.maximum, levels + ([more[2]] if more else []))
        weights = [jnp.where(x > NONE + 20.0, jnp.exp(x - peak), 0.0) for x in levels]
        total = sum(weights)
        factors = [w * jnp.exp(size) * (1.0 / CODES) for w, size in zip(weights, sizes)]
        shift = sum(factors) * 32768.0
        upper, lower = -shift, -shift
        if more:
            weight = jnp.exp(more[2] - peak)
            total = total + weight
            upper, lower = weight * more[0] - shift, weight * more[1] - shift
        for factor, x in zip(factors, sources):
            words = x[32 * r:32 * r + 32]
            upper = upper + factor * lax.shift_right_logical(words, 16).astype(jnp.float32)
            lower = lower + factor * (words & 65535).astype(jnp.float32)
        total = jnp.maximum(total, 1e-30)
        inverse = 1.0 / total
        return upper * inverse, lower * inverse, jnp.maximum(peak + jnp.log(total), NONE)

    def softmax(n):
        dz, dy = offsets(n)
        owner_at = behind(n)
        a, b = tab[0, owner_at * 2] & 31, tab[0, owner_at * 2 + 1] & 31
        first_a, second_a, first_b, second_b = tab[1, a], tab[2, a], tab[1, b], tab[2, b]
        codes = (
            jnp.where(first_a > 0, first_a, first_b),
            jnp.where(second_a > 0, second_a, jnp.where(first_a > 0, first_b, second_b)),
        )
        rows = (jnp.where(first_a > 0, 0, 1), jnp.where(second_a > 0, 0, 1))
        found = []
        for code, row in zip(codes, rows):
            q = jnp.where(row == 1, q_all[n, 1], q_all[n, 0])
            found.append((row, *page_part(code & 15, lax.shift_right_logical(code, 4), q)))
        values = []
        for r in range(2):
            tops = [jnp.where(row == r, top, LOW) for row, top, _, _ in found]
            peak = jnp.maximum(tops[0], tops[1])
            factors = [jnp.where(row == r, jnp.exp(t - peak), 0.0) for t, (row, _, _, _) in zip(tops, found)]
            total = jnp.maximum(factors[0] * found[0][2] + factors[1] * found[1][2], 1e-30)
            inverse = 1.0 / total
            value = (factors[0] * inverse) * found[0][3] + (factors[1] * inverse) * found[1][3]
            values.append((value, jnp.maximum(peak + jnp.log(total), NONE)))
        for h in range(2):
            part_send[h, dz * 4 + dy] = encode(
                [(v[32 * h:32 * h + 32], v[64 + 32 * h:96 + 32 * h], level) for v, level in values]
            )

    fetch_pool.wait()
    fill_tab.wait()

    def lightning_pair(p, carry):
        for n in (2 * p, 2 * p + 1):
            lightning(n)
        for n in (2 * p, 2 * p + 1):

            @pl.when(n > 0)
            def _(n=n):
                lin_back(n).start()

        return carry

    def pair(p, carry):
        for n in (2 * p, 2 * p + 1):
            dz, dy = offsets(n)

            @pl.when(dy > 0)
            def _(n=n):
                half(0, 0, n, at_offset(1, 0)).wait_recv()

            @pl.when(dz > 0)
            def _(n=n):
                half(1, 0, n, at_offset(1, 0)).wait_recv()

        for n in (2 * p, 2 * p + 1):
            softmax(n)
        for n in (2 * p, 2 * p + 1):
            dz, dy = offsets(n)

            @pl.when(dz > 0)
            def _(dz=dz, dy=dy):
                part(0, dz, dy).start()

            @pl.when(dy > 0)
            def _(dz=dz, dy=dy):
                part(1, dz, dy).start()

        return carry

    lax.fori_loop(0, 8, pair, 0)
    own_last.wait()
    for copy in lasts:
        copy.wait_recv()
    fetch_state.wait()
    lax.fori_loop(0, 8, lightning_pair, 0)

    def middle(k, carry):
        d = jnp.where(k < 3, 1 + 2 * k - 3 * (k // 2), 0)
        for h in range(2):
            for e in range(1, 4):
                part(h, e if h == 0 else d, d if h == 0 else e).wait_recv()
        for h in range(2):
            sources = [part_send[h, d if h == 0 else d * 4]]
            sources += [part_in[h, e * 4 + d if h == 0 else d * 4 + e] for e in range(1, 4)]
            mid_send[h, d] = encode([merged(sources, r) for r in range(2)])

        @pl.when(d > 0)
        def _():
            for h in range(2):
                last(h, d).start()

        return carry

    lax.fori_loop(0, 4, middle, 0)

    def place(n, carry):
        lin_back(n).wait_recv()
        dz, dy = offsets(n)
        rows = pl.ds(pl.multiple_of(at_offset(dz, dy) * 8, 8), 8)
        for r in range(2):
            lin_out[r, rows] = lin_in[n, r]
        return carry

    for r in range(2):
        lin_out[r, pl.ds(pl.multiple_of(me * 8, 8), 8)] = lin_send[0, r]
    lax.fori_loop(1, N, place, 0)
    for r in range(2):
        y = lin_fresh[2] * lin_out[r] + lin_fresh[r]
        lin_ref[r] = y / jnp.sqrt(jnp.mean(y * y, axis=1, keepdims=True) + 1e-5)

    for h in range(2):
        for d in DIST:
            last(h, d).wait_recv()
    for r in range(2):
        pieces = []
        for h in range(2):
            value, level = fresh[r], fresh_log[r:r + 1]
            sources = [mid_send[h, 0]] + [mid_in[h, d] for d in DIST]
            pieces.append(merged(sources, r, (value[32 * h:32 * h + 32], value[64 + 32 * h:96 + 32 * h], level)))
        soft_ref[r] = jnp.concatenate([pieces[0][0], pieces[1][0], pieces[0][1], pieces[1][1]], axis=0).T

    def finish(n, carry):
        half(0, 0, n, at_offset(1, 0)).wait_send()
        half(1, 0, n, at_offset(1, 0)).wait_send()
        lin_back(n).wait_send()
        dz, dy = offsets(n)

        @pl.when(dz > 0)
        def _():
            part(0, dz, dy).wait_send()

        @pl.when(dy > 0)
        def _():
            part(1, dz, dy).wait_send()

        return carry

    lax.fori_loop(1, N, finish, 0)
    for copy in mids + lasts + [last(h, d) for h in range(2) for d in DIST]:
        copy.wait_send()


def copy_kernel(a_ref, b_ref, c_ref, d_ref):
    c_ref[...] = a_ref[...]
    d_ref[...] = b_ref[...]


def rows_first(x):
    return x.reshape(2, 2, 64, WIDTH).transpose(0, 2, 1, 3).reshape(2, WIDTH, WIDTH)


def pairs_first(x):
    return x.reshape(2, 2, 2, 64, WIDTH).transpose(0, 1, 3, 2, 4).reshape(2, 2, WIDTH, WIDTH)


def rows_last(x):
    return x.reshape(2, 64, 2, WIDTH).transpose(0, 2, 1, 3).reshape(2, 2, 64 * WIDTH)


def shards(
    request_owner, page_list, context_len, lin_state, decay_rate, lin_query, lin_keyval, soft_query, new_keyval,
    page_pool,
):
    vmem = pl.BlockSpec(memory_space=pltpu.VMEM)
    hbm = pl.BlockSpec(memory_space=pl.ANY)
    out = [jax.ShapeDtypeStruct((2, WIDTH, WIDTH), jnp.float32)] * 2
    lin, soft = pl.pallas_call(
        kernel,
        out_shape=[pltpu.VMEM((2, WIDTH, WIDTH), jnp.float32)] * 2,
        in_specs=[hbm] * 10,
        out_specs=[vmem] * 2,
        scratch_shapes=[
            pltpu.VMEM(lin_state.shape, jnp.float32),
            pltpu.VMEM(page_pool.shape, jnp.bfloat16),
            pltpu.VMEM((1, 32), jnp.int32),
            pltpu.VMEM((8, 32), jnp.int32),
            pltpu.VMEM((1, 32), jnp.int32),
            pltpu.VMEM((1, 64), jnp.float32),
            pltpu.VMEM((2, WIDTH, WIDTH), jnp.bfloat16),
            pltpu.VMEM(new_keyval.shape, jnp.bfloat16),
            pltpu.VMEM((2, WIDTH, WIDTH), jnp.bfloat16),
            pltpu.VMEM((2, 2, WIDTH, WIDTH), jnp.bfloat16),
            pltpu.VMEM((3, WIDTH, WIDTH), jnp.float32),
            pltpu.VMEM((2, WIDTH, WIDTH), jnp.float32),
            pltpu.VMEM((2, WIDTH, WIDTH), jnp.float32),
            pltpu.VMEM((8, WIDTH), jnp.float32),
            pltpu.VMEM((N, 2, WIDTH, WIDTH), jnp.bfloat16),
            pltpu.VMEM((4, 4, 16, WIDTH), jnp.bfloat16),
            pltpu.VMEM((4, 4, 16, WIDTH), jnp.bfloat16),
            pltpu.VMEM((4, 4, 16, WIDTH), jnp.bfloat16),
            pltpu.VMEM((N, 2, 8, WIDTH), jnp.float32),
            pltpu.VMEM((N, 2, 8, WIDTH), jnp.float32),
            pltpu.VMEM((2, N, 68, WIDTH), jnp.int32),
            pltpu.VMEM((2, N, 68, WIDTH), jnp.int32),
            pltpu.VMEM((2, 4, 68, WIDTH), jnp.int32),
            pltpu.VMEM((2, 4, 68, WIDTH), jnp.int32),
            pltpu.VMEM((8, WIDTH), jnp.int32),
            pltpu.SMEM((8, WIDTH), jnp.int32),
            pltpu.SemaphoreType.DMA((13,)),
            pltpu.SemaphoreType.DMA((2, N)),
            pltpu.SemaphoreType.DMA((2, N)),
            pltpu.SemaphoreType.DMA((2, 4)),
            pltpu.SemaphoreType.DMA((2, 4)),
            pltpu.SemaphoreType.DMA((N,)),
            pltpu.SemaphoreType.DMA((N,)),
            pltpu.SemaphoreType.DMA((2, N)),
            pltpu.SemaphoreType.DMA((2, N)),
            pltpu.SemaphoreType.DMA((2, 4)),
            pltpu.SemaphoreType.DMA((2, 4)),
        ],
        compiler_params=pltpu.CompilerParams(
            collective_id=0, has_side_effects=True, vmem_limit_bytes=56 * 1024 * 1024
        ),
    )(
        request_owner.reshape(1, 32), page_list.T, context_len.reshape(1, 32), decay_rate.reshape(1, 64),
        rows_first(soft_query), new_keyval, rows_first(lin_query), pairs_first(lin_keyval), lin_state, page_pool,
    )
    lin, soft = (pltpu.with_memory_space_constraint(x, pltpu.VMEM) for x in (lin, soft))
    lin, soft = pl.pallas_call(copy_kernel, out_shape=out, in_specs=[vmem] * 2, out_specs=[vmem] * 2)(lin, soft)
    return rows_last(lin), rows_last(soft)


def solution(mesh):
    return jax.shard_map(
        shards,
        mesh=mesh,
        in_specs=(
            P("grp"), P("grp", None), P("grp"), P("grp", "head", None, None), P(),
            P(("grp", "head"), None, None), P(("grp", "head"), None, None, None),
            P(("grp", "head"), None, None), P(("grp", "head"), None, None, None),
            P(("grp", "head"), None, None, None),
        ),
        out_specs=(P(("grp", "head"), None, None), P(("grp", "head"), None, None)),
        check_vma=False,
    )
```

```python
import functools
import math

import jax
import jax.numpy as jnp
from jax import lax
from jax.experimental import pallas as pl
from jax.experimental.pallas import tpu as pltpu
from jax.sharding import PartitionSpec as P

MESH = pl.DeviceIdType.MESH
N = 16
WIDTH = 128
KVH = 8
CODES = 32000.0
LOW = -1e30
NONE = -505.0
LEVEL_UNIT = 2.0**22
SIZE_UNIT = 2.0**16
SCALE = 1.0 / math.sqrt(128.0)


DIST = (1, 3, 2)
OFFSETS = ((0, 0), (1, 0), (0, 1), (3, 0), (0, 3), (2, 0), (0, 2), (1, 1), (1, 3), (3, 1), (1, 2), (2, 1), (3, 3), (3, 2), (2, 3), (2, 2))
SLOT = {offset: n for n, offset in enumerate(OFFSETS)}


def packed(axis):
    bits = sum(offset[axis] << 2 * n for n, offset in enumerate(OFFSETS))
    return bits - (1 << 32) if bits >= 1 << 31 else bits


def offsets(n):
    return tuple(lax.shift_right_logical(jnp.int32(packed(axis)), jnp.int32(2 * n)) & 3 for axis in (0, 1))


def make_tables(owner, pages, length, me):
    sub = lax.broadcasted_iota(jnp.int32, (32, 32), 0)
    lane = lax.broadcasted_iota(jnp.int32, (32, 32), 1)

    def column(row):
        return jnp.sum(jnp.where(sub == lane, row, 0), axis=1, keepdims=True)

    slot = jnp.sum(jnp.where((column(owner) == owner) & (sub < lane), 1, 0), axis=0, keepdims=True)
    row = owner * 2 + slot
    request_of = jnp.sum(jnp.where(column(row) == lane, sub, 0), axis=0, keepdims=True)
    j = lax.broadcasted_iota(jnp.int32, (8, 32), 0)
    count = jnp.clip(length - j * WIDTH, 0, WIDTH)
    here = (lax.shift_right_logical(pages, 4) == me) & (count > 0)
    code = (pages & 15) + count * 16
    least = jnp.min(jnp.where(here, j, 8), axis=0, keepdims=True)
    most = jnp.max(jnp.where(here, j, -1), axis=0, keepdims=True)
    first = jnp.sum(jnp.where(here & (j == least), code, 0), axis=0, keepdims=True)
    second = jnp.sum(jnp.where(here & (j == most) & (most != least), code, 0), axis=0, keepdims=True)
    return request_of, first, second


def kernel(
    owner_hbm, pages_hbm, length_hbm, rate_hbm, sq_hbm, nkv_hbm, lq_hbm, lkv_hbm, state_hbm, pool_hbm, lin_ref, soft_ref,
    state, pool, owner, pages, length, rate, sq, nkv, lq, lkv, lin_fresh, lin_out, fresh, fresh_log, q_all, lin_pack, lin_mid, lin_all, lin_send, lin_in, part_send, part_in, mid_send, mid_in,
    tab_rows, tab, local_sem, half_send, half_recv, mid_sems, mid_recvs, back_send, back_recv,
    part_sems, part_recvs, last_sems, last_recvs,
):
    me = lax.axis_index("head")
    mz, my = me // 4, me % 4

    def at_offset(dz, dy):
        return (mz + dz) % 4 * 4 + (my + dy) % 4

    def behind(n):
        dz, dy = offsets(n)
        return at_offset(4 - dz, 4 - dy)

    def remote(src, dst, send, recv, to):
        return pltpu.make_async_remote_copy(
            src_ref=src, dst_ref=dst, send_sem=send, recv_sem=recv, device_id={"head": to}, device_id_type=MESH
        )

    def half(h, src, dst, to):
        rows = pl.ds(64 * h, 64)
        return remote(
            q_all.at[src, :, rows], q_all.at[dst, :, rows], half_send.at[h, dst], half_recv.at[h, dst], to
        )

    def lin_back(n):
        return remote(lin_send.at[n], lin_in.at[n], back_send.at[n], back_recv.at[n], behind(n))

    def part(h, dz, dy):
        to = at_offset(4 - dz, 0) if h == 0 else at_offset(0, 4 - dy)
        n = dz * 4 + dy
        return remote(part_send.at[h, n], part_in.at[h, n], part_sems.at[h, n], part_recvs.at[h, n], to)

    def last(h, d):
        to = at_offset(0, 4 - d) if h == 0 else at_offset(4 - d, 0)
        return remote(mid_send.at[h, d], mid_in.at[h, d], last_sems.at[h, d], last_recvs.at[h, d], to)

    barrier = pltpu.get_barrier_semaphore()
    for d in DIST:
        for to in (at_offset(d, 0), at_offset(0, d)):
            pl.semaphore_signal(barrier, inc=1, device_id={"head": to}, device_id_type=MESH)
    loads = [
        pltpu.make_async_copy(src, dst, local_sem.at[5 + n])
        for n, (src, dst) in enumerate(
            (
                (owner_hbm, owner), (pages_hbm, pages), (length_hbm, length), (rate_hbm, rate),
                (sq_hbm, sq), (lq_hbm, lq), (lkv_hbm, lkv), (nkv_hbm, nkv),
            )
        )
    ]
    for copy in loads:
        copy.start()
    fetch_pool = pltpu.make_async_copy(pool_hbm, pool, local_sem.at[1])
    fetch_state = pltpu.make_async_copy(state_hbm, state, local_sem.at[0])
    fetch_pool.start()
    fetch_state.start()
    for copy in loads:
        copy.wait()
    tab_rows[...] = jnp.zeros((8, WIDTH), jnp.int32)
    for n, row in enumerate(make_tables(owner[...], pages[...], length[...], me)):
        tab_rows[n:n + 1, 0:32] = row
    fill_tab = pltpu.make_async_copy(tab_rows, tab, local_sem.at[4])
    fill_tab.start()
    wide = [lq[r].astype(jnp.float32) for r in range(2)]
    for peer in range(N):
        lin_pack[peer // 4, peer % 4] = jnp.concatenate(
            [x[peer * 8:peer * 8 + 8] for x in wide], axis=0
        ).astype(jnp.bfloat16)
    own_mid = pltpu.make_async_copy(lin_pack.at[mz], lin_mid.at[0], local_sem.at[2])
    own_mid.start()
    for r in range(2):
        q_all[0, r] = sq[r].astype(jnp.float32).T.astype(jnp.bfloat16)

    row_of = lax.broadcasted_iota(jnp.int32, (WIDTH, 64), 0)
    lane_of = lax.broadcasted_iota(jnp.int32, (WIDTH, 64), 1)
    rates = jnp.sum(jnp.where(lane_of == row_of // 2, rate[...], 0.0), axis=1, keepdims=True)
    second = lax.broadcasted_iota(jnp.int32, (WIDTH, 1), 0) % 2 == 1
    lam = jnp.exp(-rates)
    lam_state = jnp.where(second, lam * lam, lam)
    lam_first = jnp.where(second, lam, 1.0)
    lam_second = jnp.where(second, 1.0, 0.0)
    odd = lax.broadcasted_iota(jnp.int32, (WIDTH, WIDTH), 0) % 2 == 1

    def keys_values(x):
        return jnp.where(odd, pltpu.roll(x, 1, 0), x), jnp.where(odd, x, pltpu.roll(x, WIDTH - 1, 0))

    for r in range(2):
        k1, v1 = keys_values(lkv[r, 0].astype(jnp.float32))
        k2, v2 = keys_values(lkv[r, 1].astype(jnp.float32))
        qk1 = jnp.sum(wide[r] * k1, axis=1, keepdims=True)
        qk2 = jnp.sum(wide[r] * k2, axis=1, keepdims=True)
        lin_fresh[r] = (lam_first * qk1) * v1 + (lam_second * qk2) * v2
    lin_fresh[2] = jnp.broadcast_to(lam_state, (WIDTH, WIDTH))
    step = lax.broadcasted_iota(jnp.int32, (1, WIDTH), 1) % 2

    def by_head(x):
        return jnp.concatenate(
            [jnp.broadcast_to(x[:, c * WIDTH:(c + 1) * WIDTH], (16, WIDTH)) for c in range(KVH)], axis=0
        ).T

    for r in range(2):
        q = q_all[0, r].astype(jnp.float32)
        kv = [nkv[r, t].astype(jnp.float32) for t in range(2)]
        s0 = jnp.sum(q * by_head(kv[0][0:1]), axis=0, keepdims=True) * SCALE
        s1 = jnp.sum(q * by_head(kv[1][0:1]), axis=0, keepdims=True) * SCALE
        top = jnp.where(step == 1, jnp.maximum(s0, s1), s0)
        w0 = jnp.exp(s0 - top)
        w1 = jnp.where(step == 1, jnp.exp(s1 - top), 0.0)
        r0 = w0.astype(jnp.bfloat16).astype(jnp.float32)
        r1 = w1.astype(jnp.bfloat16).astype(jnp.float32)
        fresh[r] = (r0 * by_head(kv[0][1:2]) + r1 * by_head(kv[1][1:2])) / (w0 + w1)
        fresh_log[r:r + 1] = top + jnp.log(w0 + w1)
    pl.semaphore_wait(barrier, 6)

    mids = [
        remote(lin_pack.at[(mz + d) % 4], lin_mid.at[d], mid_sems.at[0, d], mid_recvs.at[0, d], at_offset(d, 0))
        for d in DIST
    ]
    for copy in mids:
        copy.start()

    first = {}
    for d in DIST:
        first[0, d] = half(0, 0, SLOT[d, 0], at_offset(d, 0))
        first[1, d] = half(1, 0, SLOT[0, d], at_offset(0, d))
    for copy in first.values():
        copy.start()
    for d in DIST:
        half(0, 0, SLOT[0, d], at_offset(0, d)).start()
        half(1, 0, SLOT[d, 0], at_offset(d, 0)).start()
    own_mid.wait()
    for copy in mids:
        copy.wait_recv()
    lasts = [
        remote(
            lin_mid.at[:, (my + d) % 4], lin_all.at[d], mid_sems.at[1, d], mid_recvs.at[1, d], at_offset(0, d)
        )
        for d in DIST
    ]
    for copy in lasts:
        copy.start()
    own_last = pltpu.make_async_copy(lin_mid.at[:, my], lin_all.at[0], local_sem.at[3])
    own_last.start()
    here = set()
    for dz, dy in OFFSETS[7:]:
        for h, d in ((0, dz), (1, dy)):
            if (h, d) not in here:
                first[h, d].wait_recv()
                here.add((h, d))
        half(0, SLOT[dz, 0], SLOT[dz, dy], at_offset(0, dy)).start()
        half(1, SLOT[0, dy], SLOT[dz, dy], at_offset(dz, 0)).start()

    head_of = lax.broadcasted_iota(jnp.int32, (8, WIDTH), 0) // 2

    def lightning(n):
        dz, dy = offsets(n)
        owner_at = behind(n)
        block = lin_all[dy, dz].astype(jnp.float32)
        for r in range(2):
            request = tab[0, owner_at * 2 + r] & 31
            q = block[8 * r:8 * r + 8].astype(jnp.bfloat16)
            q_two = jnp.concatenate([q, q], axis=1)
            y = jnp.zeros((8, WIDTH), jnp.float32)
            for h in range(4):
                s = state[request, h]
                high = s.astype(jnp.bfloat16)
                low = (s - high.astype(jnp.float32)).astype(jnp.bfloat16)
                got = jnp.dot(q_two, jnp.concatenate([high, low], axis=0), preferred_element_type=jnp.float32)
                y = jnp.where(head_of == h, got, y)
            lin_send[n, r] = y

    position = lax.broadcasted_iota(jnp.int32, (WIDTH, WIDTH), 0)
    lane_head = lax.broadcasted_iota(jnp.int32, (WIDTH, WIDTH), 1) // 16
    of_head = [jnp.where(lane_head == c, 1.0, 0.0).astype(jnp.bfloat16) for c in range(KVH)]

    def page_part(page, count, q):
        scores = sum(
            jnp.dot(
                pool[page, 0, :, c * WIDTH:(c + 1) * WIDTH], q * of_head[c], preferred_element_type=jnp.float32
            )
            for c in range(KVH)
        ) * SCALE
        live = position < count
        top = jnp.max(jnp.where(live, scores, LOW), axis=0, keepdims=True)
        weight = jnp.where(live, jnp.exp(scores - top), 0.0)
        total = jnp.sum(weight, axis=0, keepdims=True)
        rounded = weight.astype(jnp.bfloat16)
        acc = sum(
            lax.dot_general(
                pool[page, 1, :, c * WIDTH:(c + 1) * WIDTH], rounded * of_head[c], (((0,), (0,)), ((), ())),
                preferred_element_type=jnp.float32,
            )
            for c in range(KVH)
        )
        return top, total, acc

    def encode(found):
        words, logs = [], []
        for upper, lower, level in found:
            most = jnp.maximum(
                jnp.max(jnp.abs(upper), axis=0, keepdims=True), jnp.max(jnp.abs(lower), axis=0, keepdims=True)
            )
            size = jnp.ceil(jnp.log(jnp.maximum(most, 1e-30)) * SIZE_UNIT)
            inverse = CODES * jnp.exp(size * (-1.0 / SIZE_UNIT))
            high = (upper * inverse + 32768.5).astype(jnp.int32)
            low = (lower * inverse + 32768.5).astype(jnp.int32)
            words.append(lax.shift_left(high, 16) | low)
            logs += [(level * LEVEL_UNIT).astype(jnp.int32), size.astype(jnp.int32)]
        return jnp.concatenate(words + logs, axis=0)

    def merged(sources, r, more=None):
        levels = [x[64 + 2 * r:65 + 2 * r].astype(jnp.float32) * (1.0 / LEVEL_UNIT) for x in sources]
        sizes = [x[65 + 2 * r:66 + 2 * r].astype(jnp.float32) * (1.0 / SIZE_UNIT) for x in sources]
        peak = functools.reduce(jnp.maximum, levels + ([more[2]] if more else []))
        weights = [jnp.where(x > NONE + 20.0, jnp.exp(x - peak), 0.0) for x in levels]
        total = sum(weights)
        factors = [w * jnp.exp(size) * (1.0 / CODES) for w, size in zip(weights, sizes)]
        shift = sum(factors) * 32768.0
        upper, lower = -shift, -shift
        if more:
            weight = jnp.exp(more[2] - peak)
            total = total + weight
            upper, lower = weight * more[0] - shift, weight * more[1] - shift
        for factor, x in zip(factors, sources):
            words = x[32 * r:32 * r + 32]
            upper = upper + factor * lax.shift_right_logical(words, 16).astype(jnp.float32)
            lower = lower + factor * (words & 65535).astype(jnp.float32)
        total = jnp.maximum(total, 1e-30)
        inverse = 1.0 / total
        return upper * inverse, lower * inverse, jnp.maximum(peak + jnp.log(total), NONE)

    def softmax(n):
        dz, dy = offsets(n)
        owner_at = behind(n)
        a, b = tab[0, owner_at * 2] & 31, tab[0, owner_at * 2 + 1] & 31
        first_a, second_a, first_b, second_b = tab[1, a], tab[2, a], tab[1, b], tab[2, b]
        codes = (
            jnp.where(first_a > 0, first_a, first_b),
            jnp.where(second_a > 0, second_a, jnp.where(first_a > 0, first_b, second_b)),
        )
        rows = (jnp.where(first_a > 0, 0, 1), jnp.where(second_a > 0, 0, 1))
        found = []
        for code, row in zip(codes, rows):
            q = jnp.where(row == 1, q_all[n, 1], q_all[n, 0])
            found.append((row, *page_part(code & 15, lax.shift_right_logical(code, 4), q)))
        values = []
        for r in range(2):
            tops = [jnp.where(row == r, top, LOW) for row, top, _, _ in found]
            peak = jnp.maximum(tops[0], tops[1])
            factors = [jnp.where(row == r, jnp.exp(t - peak), 0.0) for t, (row, _, _, _) in zip(tops, found)]
            total = jnp.maximum(factors[0] * found[0][2] + factors[1] * found[1][2], 1e-30)
            inverse = 1.0 / total
            value = (factors[0] * inverse) * found[0][3] + (factors[1] * inverse) * found[1][3]
            values.append((value, jnp.maximum(peak + jnp.log(total), NONE)))
        for h in range(2):
            part_send[h, dz * 4 + dy] = encode(
                [(v[32 * h:32 * h + 32], v[64 + 32 * h:96 + 32 * h], level) for v, level in values]
            )

    fetch_pool.wait()
    fill_tab.wait()

    def lightning_pair(p, carry):
        for n in (2 * p, 2 * p + 1):
            lightning(n)
        for n in (2 * p, 2 * p + 1):

            @pl.when(n > 0)
            def _(n=n):
                lin_back(n).start()

        return carry

    def pair(p, carry):
        for n in (2 * p, 2 * p + 1):
            dz, dy = offsets(n)

            @pl.when(dy > 0)
            def _(n=n):
                half(0, 0, n, at_offset(1, 0)).wait_recv()

            @pl.when(dz > 0)
            def _(n=n):
                half(1, 0, n, at_offset(1, 0)).wait_recv()

        for n in (2 * p, 2 * p + 1):
            softmax(n)
        for n in (2 * p, 2 * p + 1):
            dz, dy = offsets(n)

            @pl.when(dz > 0)
            def _(dz=dz, dy=dy):
                part(0, dz, dy).start()

            @pl.when(dy > 0)
            def _(dz=dz, dy=dy):
                part(1, dz, dy).start()

        return carry

    lax.fori_loop(0, 8, pair, 0)
    own_last.wait()
    for copy in lasts:
        copy.wait_recv()
    fetch_state.wait()
    lax.fori_loop(0, 8, lightning_pair, 0)

    def middle(k, carry):
        d = jnp.where(k < 3, 1 + 2 * k - 3 * (k // 2), 0)
        for h in range(2):
            for e in range(1, 4):
                part(h, e if h == 0 else d, d if h == 0 else e).wait_recv()
            sources = [part_send[h, d if h == 0 else d * 4]]
            sources += [part_in[h, e * 4 + d if h == 0 else d * 4 + e] for e in range(1, 4)]
            mid_send[h, d] = encode([merged(sources, r) for r in range(2)])

            @pl.when(d > 0)
            def _(h=h):
                last(h, d).start()

        return carry

    lax.fori_loop(0, 4, middle, 0)

    def place(n, carry):
        lin_back(n).wait_recv()
        dz, dy = offsets(n)
        rows = pl.ds(pl.multiple_of(at_offset(dz, dy) * 8, 8), 8)
        for r in range(2):
            lin_out[r, rows] = lin_in[n, r]
        return carry

    for r in range(2):
        lin_out[r, pl.ds(pl.multiple_of(me * 8, 8), 8)] = lin_send[0, r]
    lax.fori_loop(1, N, place, 0)
    for r in range(2):
        y = lin_fresh[2] * lin_out[r] + lin_fresh[r]
        lin_ref[r] = y / jnp.sqrt(jnp.mean(y * y, axis=1, keepdims=True) + 1e-5)

    def finish(n, carry):
        half(0, 0, n, at_offset(1, 0)).wait_send()
        half(1, 0, n, at_offset(1, 0)).wait_send()
        lin_back(n).wait_send()
        dz, dy = offsets(n)

        @pl.when(dz > 0)
        def _():
            part(0, dz, dy).wait_send()

        @pl.when(dy > 0)
        def _():
            part(1, dz, dy).wait_send()

        return carry

    lax.fori_loop(1, N, finish, 0)
    for copy in mids + lasts:
        copy.wait_send()

    for h in range(2):
        for d in DIST:
            last(h, d).wait_recv()
    for r in range(2):
        pieces = []
        for h in range(2):
            value, level = fresh[r], fresh_log[r:r + 1]
            sources = [mid_send[h, 0]] + [mid_in[h, d] for d in DIST]
            pieces.append(merged(sources, r, (value[32 * h:32 * h + 32], value[64 + 32 * h:96 + 32 * h], level)))
        soft_ref[r] = jnp.concatenate([pieces[0][0], pieces[1][0], pieces[0][1], pieces[1][1]], axis=0).T
    for copy in [last(h, d) for h in range(2) for d in DIST]:
        copy.wait_send()


def copy_kernel(a_ref, b_ref, c_ref, d_ref):
    c_ref[...] = a_ref[...]
    d_ref[...] = b_ref[...]


def rows_first(x):
    return x.reshape(2, 2, 64, WIDTH).transpose(0, 2, 1, 3).reshape(2, WIDTH, WIDTH)


def pairs_first(x):
    return x.reshape(2, 2, 2, 64, WIDTH).transpose(0, 1, 3, 2, 4).reshape(2, 2, WIDTH, WIDTH)


def rows_last(x):
    return x.reshape(2, 64, 2, WIDTH).transpose(0, 2, 1, 3).reshape(2, 2, 64 * WIDTH)


def shards(
    request_owner, page_list, context_len, lin_state, decay_rate, lin_query, lin_keyval, soft_query, new_keyval,
    page_pool,
):
    vmem = pl.BlockSpec(memory_space=pltpu.VMEM)
    hbm = pl.BlockSpec(memory_space=pl.ANY)
    out = [jax.ShapeDtypeStruct((2, WIDTH, WIDTH), jnp.float32)] * 2
    lin, soft = pl.pallas_call(
        kernel,
        out_shape=[pltpu.VMEM((2, WIDTH, WIDTH), jnp.float32)] * 2,
        in_specs=[hbm] * 10,
        out_specs=[vmem] * 2,
        scratch_shapes=[
            pltpu.VMEM(lin_state.shape, jnp.float32),
            pltpu.VMEM(page_pool.shape, jnp.bfloat16),
            pltpu.VMEM((1, 32), jnp.int32),
            pltpu.VMEM((8, 32), jnp.int32),
            pltpu.VMEM((1, 32), jnp.int32),
            pltpu.VMEM((1, 64), jnp.float32),
            pltpu.VMEM((2, WIDTH, WIDTH), jnp.bfloat16),
            pltpu.VMEM(new_keyval.shape, jnp.bfloat16),
            pltpu.VMEM((2, WIDTH, WIDTH), jnp.bfloat16),
            pltpu.VMEM((2, 2, WIDTH, WIDTH), jnp.bfloat16),
            pltpu.VMEM((3, WIDTH, WIDTH), jnp.float32),
            pltpu.VMEM((2, WIDTH, WIDTH), jnp.float32),
            pltpu.VMEM((2, WIDTH, WIDTH), jnp.float32),
            pltpu.VMEM((8, WIDTH), jnp.float32),
            pltpu.VMEM((N, 2, WIDTH, WIDTH), jnp.bfloat16),
            pltpu.VMEM((4, 4, 16, WIDTH), jnp.bfloat16),
            pltpu.VMEM((4, 4, 16, WIDTH), jnp.bfloat16),
            pltpu.VMEM((4, 4, 16, WIDTH), jnp.bfloat16),
            pltpu.VMEM((N, 2, 8, WIDTH), jnp.float32),
            pltpu.VMEM((N, 2, 8, WIDTH), jnp.float32),
            pltpu.VMEM((2, N, 68, WIDTH), jnp.int32),
            pltpu.VMEM((2, N, 68, WIDTH), jnp.int32),
            pltpu.VMEM((2, 4, 68, WIDTH), jnp.int32),
            pltpu.VMEM((2, 4, 68, WIDTH), jnp.int32),
            pltpu.VMEM((8, WIDTH), jnp.int32),
            pltpu.SMEM((8, WIDTH), jnp.int32),
            pltpu.SemaphoreType.DMA((13,)),
            pltpu.SemaphoreType.DMA((2, N)),
            pltpu.SemaphoreType.DMA((2, N)),
            pltpu.SemaphoreType.DMA((2, 4)),
            pltpu.SemaphoreType.DMA((2, 4)),
            pltpu.SemaphoreType.DMA((N,)),
            pltpu.SemaphoreType.DMA((N,)),
            pltpu.SemaphoreType.DMA((2, N)),
            pltpu.SemaphoreType.DMA((2, N)),
            pltpu.SemaphoreType.DMA((2, 4)),
            pltpu.SemaphoreType.DMA((2, 4)),
        ],
        compiler_params=pltpu.CompilerParams(
            collective_id=0, has_side_effects=True, vmem_limit_bytes=56 * 1024 * 1024
        ),
    )(
        request_owner.reshape(1, 32), page_list.T, context_len.reshape(1, 32), decay_rate.reshape(1, 64),
        rows_first(soft_query), new_keyval, rows_first(lin_query), pairs_first(lin_keyval), lin_state, page_pool,
    )
    lin, soft = (pltpu.with_memory_space_constraint(x, pltpu.VMEM) for x in (lin, soft))
    lin, soft = pl.pallas_call(copy_kernel, out_shape=out, in_specs=[vmem] * 2, out_specs=[vmem] * 2)(lin, soft)
    return rows_last(lin), rows_last(soft)


def solution(mesh):
    return jax.shard_map(
        shards,
        mesh=mesh,
        in_specs=(
            P("grp"), P("grp", None), P("grp"), P("grp", "head", None, None), P(),
            P(("grp", "head"), None, None), P(("grp", "head"), None, None, None),
            P(("grp", "head"), None, None), P(("grp", "head"), None, None, None),
            P(("grp", "head"), None, None, None),
        ),
        out_specs=(P(("grp", "head"), None, None), P(("grp", "head"), None, None)),
        check_vma=False,
    )
```

```python
import functools
import math

import jax
import jax.numpy as jnp
from jax import lax
from jax.experimental import pallas as pl
from jax.experimental.pallas import tpu as pltpu
from jax.sharding import PartitionSpec as P

MESH = pl.DeviceIdType.MESH
N = 16
WIDTH = 128
KVH = 8
CODES = 32000.0
LOW = -1e30
NONE = -505.0
LEVEL_UNIT = 2.0**22
SIZE_UNIT = 2.0**16
SCALE = 1.0 / math.sqrt(128.0)


DIST = (1, 3, 2)
OFFSETS = ((0, 0), (1, 0), (0, 1), (3, 0), (0, 3), (2, 0), (0, 2), (1, 1), (1, 3), (3, 1), (1, 2), (2, 1), (3, 3), (3, 2), (2, 3), (2, 2))
SLOT = {offset: n for n, offset in enumerate(OFFSETS)}


def packed(axis):
    bits = sum(offset[axis] << 2 * n for n, offset in enumerate(OFFSETS))
    return bits - (1 << 32) if bits >= 1 << 31 else bits


def offsets(n):
    return tuple(lax.shift_right_logical(jnp.int32(packed(axis)), jnp.int32(2 * n)) & 3 for axis in (0, 1))


def make_tables(owner, pages, length, me):
    sub = lax.broadcasted_iota(jnp.int32, (32, 32), 0)
    lane = lax.broadcasted_iota(jnp.int32, (32, 32), 1)

    def column(row):
        return jnp.sum(jnp.where(sub == lane, row, 0), axis=1, keepdims=True)

    slot = jnp.sum(jnp.where((column(owner) == owner) & (sub < lane), 1, 0), axis=0, keepdims=True)
    row = owner * 2 + slot
    request_of = jnp.sum(jnp.where(column(row) == lane, sub, 0), axis=0, keepdims=True)
    j = lax.broadcasted_iota(jnp.int32, (8, 32), 0)
    count = jnp.clip(length - j * WIDTH, 0, WIDTH)
    here = (lax.shift_right_logical(pages, 4) == me) & (count > 0)
    code = (pages & 15) + count * 16
    least = jnp.min(jnp.where(here, j, 8), axis=0, keepdims=True)
    most = jnp.max(jnp.where(here, j, -1), axis=0, keepdims=True)
    first = jnp.sum(jnp.where(here & (j == least), code, 0), axis=0, keepdims=True)
    second = jnp.sum(jnp.where(here & (j == most) & (most != least), code, 0), axis=0, keepdims=True)
    return request_of, first, second


def kernel(
    owner_hbm, pages_hbm, length_hbm, rate_hbm, sq_hbm, nkv_hbm, lq_hbm, lkv_hbm, state_hbm, pool_hbm, lin_ref, soft_ref,
    state, pool, owner, pages, length, rate, sq, nkv, lq, lkv, lin_fresh, lin_out, fresh, fresh_log, q_all, lin_pack, lin_mid, lin_all, lin_send, lin_in, part_send, part_in, mid_send, mid_in,
    tab_rows, tab, local_sem, half_send, half_recv, mid_sems, mid_recvs, back_send, back_recv,
    part_sems, part_recvs, last_sems, last_recvs,
):
    me = lax.axis_index("head")
    mz, my = me // 4, me % 4

    def at_offset(dz, dy):
        return (mz + dz) % 4 * 4 + (my + dy) % 4

    def behind(n):
        dz, dy = offsets(n)
        return at_offset(4 - dz, 4 - dy)

    def remote(src, dst, send, recv, to):
        return pltpu.make_async_remote_copy(
            src_ref=src, dst_ref=dst, send_sem=send, recv_sem=recv, device_id={"head": to}, device_id_type=MESH
        )

    def half(h, src, dst, to):
        rows = pl.ds(64 * h, 64)
        return remote(
            q_all.at[src, :, rows], q_all.at[dst, :, rows], half_send.at[h, dst], half_recv.at[h, dst], to
        )

    def lin_back(n):
        return remote(lin_send.at[n], lin_in.at[n], back_send.at[n], back_recv.at[n], behind(n))

    def part(h, dz, dy):
        to = at_offset(4 - dz, 0) if h == 0 else at_offset(0, 4 - dy)
        n = dz * 4 + dy
        return remote(part_send.at[h, n], part_in.at[h, n], part_sems.at[h, n], part_recvs.at[h, n], to)

    def last(h, d):
        to = at_offset(0, 4 - d) if h == 0 else at_offset(4 - d, 0)
        return remote(mid_send.at[h, d], mid_in.at[h, d], last_sems.at[h, d], last_recvs.at[h, d], to)

    barrier = pltpu.get_barrier_semaphore()
    for d in DIST:
        for to in (at_offset(d, 0), at_offset(0, d)):
            pl.semaphore_signal(barrier, inc=1, device_id={"head": to}, device_id_type=MESH)
    loads = [
        pltpu.make_async_copy(src, dst, local_sem.at[5 + n])
        for n, (src, dst) in enumerate(
            (
                (owner_hbm, owner), (pages_hbm, pages), (length_hbm, length), (rate_hbm, rate),
                (sq_hbm, sq), (lq_hbm, lq), (lkv_hbm, lkv), (nkv_hbm, nkv),
            )
        )
    ]
    for copy in loads:
        copy.start()
    fetch_pool = pltpu.make_async_copy(pool_hbm, pool, local_sem.at[1])
    fetch_state = pltpu.make_async_copy(state_hbm, state, local_sem.at[0])
    fetch_pool.start()
    fetch_state.start()
    for copy in loads:
        copy.wait()
    tab_rows[...] = jnp.zeros((8, WIDTH), jnp.int32)
    for n, row in enumerate(make_tables(owner[...], pages[...], length[...], me)):
        tab_rows[n:n + 1, 0:32] = row
    fill_tab = pltpu.make_async_copy(tab_rows, tab, local_sem.at[4])
    fill_tab.start()
    wide = [lq[r].astype(jnp.float32) for r in range(2)]
    for peer in range(N):
        lin_pack[peer // 4, peer % 4] = jnp.concatenate(
            [x[peer * 8:peer * 8 + 8] for x in wide], axis=0
        ).astype(jnp.bfloat16)
    own_mid = pltpu.make_async_copy(lin_pack.at[mz], lin_mid.at[0], local_sem.at[2])
    own_mid.start()
    for r in range(2):
        q_all[0, r] = sq[r].astype(jnp.float32).T.astype(jnp.bfloat16)

    row_of = lax.broadcasted_iota(jnp.int32, (WIDTH, 64), 0)
    lane_of = lax.broadcasted_iota(jnp.int32, (WIDTH, 64), 1)
    rates = jnp.sum(jnp.where(lane_of == row_of // 2, rate[...], 0.0), axis=1, keepdims=True)
    second = lax.broadcasted_iota(jnp.int32, (WIDTH, 1), 0) % 2 == 1
    lam = jnp.exp(-rates)
    lam_state = jnp.where(second, lam * lam, lam)
    lam_first = jnp.where(second, lam, 1.0)
    lam_second = jnp.where(second, 1.0, 0.0)
    odd = lax.broadcasted_iota(jnp.int32, (WIDTH, WIDTH), 0) % 2 == 1

    def keys_values(x):
        return jnp.where(odd, pltpu.roll(x, 1, 0), x), jnp.where(odd, x, pltpu.roll(x, WIDTH - 1, 0))

    for r in range(2):
        k1, v1 = keys_values(lkv[r, 0].astype(jnp.float32))
        k2, v2 = keys_values(lkv[r, 1].astype(jnp.float32))
        qk1 = jnp.sum(wide[r] * k1, axis=1, keepdims=True)
        qk2 = jnp.sum(wide[r] * k2, axis=1, keepdims=True)
        lin_fresh[r] = (lam_first * qk1) * v1 + (lam_second * qk2) * v2
    lin_fresh[2] = jnp.broadcast_to(lam_state, (WIDTH, WIDTH))
    step = lax.broadcasted_iota(jnp.int32, (1, WIDTH), 1) % 2

    def by_head(x):
        return jnp.concatenate(
            [jnp.broadcast_to(x[:, c * WIDTH:(c + 1) * WIDTH], (16, WIDTH)) for c in range(KVH)], axis=0
        ).T

    for r in range(2):
        q = q_all[0, r].astype(jnp.float32)
        kv = [nkv[r, t].astype(jnp.float32) for t in range(2)]
        s0 = jnp.sum(q * by_head(kv[0][0:1]), axis=0, keepdims=True) * SCALE
        s1 = jnp.sum(q * by_head(kv[1][0:1]), axis=0, keepdims=True) * SCALE
        top = jnp.where(step == 1, jnp.maximum(s0, s1), s0)
        w0 = jnp.exp(s0 - top)
        w1 = jnp.where(step == 1, jnp.exp(s1 - top), 0.0)
        r0 = w0.astype(jnp.bfloat16).astype(jnp.float32)
        r1 = w1.astype(jnp.bfloat16).astype(jnp.float32)
        fresh[r] = (r0 * by_head(kv[0][1:2]) + r1 * by_head(kv[1][1:2])) / (w0 + w1)
        fresh_log[r:r + 1] = top + jnp.log(w0 + w1)
    pl.semaphore_wait(barrier, 6)

    mids = [
        remote(lin_pack.at[(mz + d) % 4], lin_mid.at[d], mid_sems.at[0, d], mid_recvs.at[0, d], at_offset(d, 0))
        for d in DIST
    ]
    for copy in mids:
        copy.start()

    first = {}
    for d in DIST:
        first[0, d] = half(0, 0, SLOT[d, 0], at_offset(d, 0))
        first[1, d] = half(1, 0, SLOT[0, d], at_offset(0, d))
    for copy in first.values():
        copy.start()
    for d in DIST:
        half(0, 0, SLOT[0, d], at_offset(0, d)).start()
        half(1, 0, SLOT[d, 0], at_offset(d, 0)).start()
    own_mid.wait()
    for copy in mids:
        copy.wait_recv()
    lasts = [
        remote(
            lin_mid.at[:, (my + d) % 4], lin_all.at[d], mid_sems.at[1, d], mid_recvs.at[1, d], at_offset(0, d)
        )
        for d in DIST
    ]
    for copy in lasts:
        copy.start()
    own_last = pltpu.make_async_copy(lin_mid.at[:, my], lin_all.at[0], local_sem.at[3])
    own_last.start()
    here = set()
    for dz, dy in OFFSETS[7:]:
        for h, d in ((0, dz), (1, dy)):
            if (h, d) not in here:
                first[h, d].wait_recv()
                here.add((h, d))
        half(0, SLOT[dz, 0], SLOT[dz, dy], at_offset(0, dy)).start()
        half(1, SLOT[0, dy], SLOT[dz, dy], at_offset(dz, 0)).start()

    head_of = lax.broadcasted_iota(jnp.int32, (8, WIDTH), 0) // 2

    def lightning(n):
        dz, dy = offsets(n)
        owner_at = behind(n)
        block = lin_all[dy, dz].astype(jnp.float32)
        for r in range(2):
            request = tab[0, owner_at * 2 + r] & 31
            q = block[8 * r:8 * r + 8].astype(jnp.bfloat16)
            q_two = jnp.concatenate([q, q], axis=1)
            y = jnp.zeros((8, WIDTH), jnp.float32)
            for h in range(4):
                s = state[request, h]
                high = s.astype(jnp.bfloat16)
                low = (s - high.astype(jnp.float32)).astype(jnp.bfloat16)
                got = jnp.dot(q_two, jnp.concatenate([high, low], axis=0), preferred_element_type=jnp.float32)
                y = jnp.where(head_of == h, got, y)
            lin_send[n, r] = y

    position = lax.broadcasted_iota(jnp.int32, (WIDTH, WIDTH), 0)
    lane_head = lax.broadcasted_iota(jnp.int32, (WIDTH, WIDTH), 1) // 16
    of_head = [jnp.where(lane_head == c, 1.0, 0.0).astype(jnp.bfloat16) for c in range(KVH)]

    def page_part(page, count, q):
        scores = sum(
            jnp.dot(
                pool[page, 0, :, c * WIDTH:(c + 1) * WIDTH], q * of_head[c], preferred_element_type=jnp.float32
            )
            for c in range(KVH)
        ) * SCALE
        live = position < count
        top = jnp.max(jnp.where(live, scores, LOW), axis=0, keepdims=True)
        weight = jnp.where(live, jnp.exp(scores - top), 0.0)
        total = jnp.sum(weight, axis=0, keepdims=True)
        rounded = weight.astype(jnp.bfloat16)
        acc = sum(
            lax.dot_general(
                pool[page, 1, :, c * WIDTH:(c + 1) * WIDTH], rounded * of_head[c], (((0,), (0,)), ((), ())),
                preferred_element_type=jnp.float32,
            )
            for c in range(KVH)
        )
        return top, total, acc

    def encode(found):
        words, logs = [], []
        for upper, lower, level in found:
            most = jnp.maximum(
                jnp.max(jnp.abs(upper), axis=0, keepdims=True), jnp.max(jnp.abs(lower), axis=0, keepdims=True)
            )
            size = jnp.ceil(jnp.log(jnp.maximum(most, 1e-30)) * SIZE_UNIT)
            inverse = CODES * jnp.exp(size * (-1.0 / SIZE_UNIT))
            high = (upper * inverse + 32768.5).astype(jnp.int32)
            low = (lower * inverse + 32768.5).astype(jnp.int32)
            words.append(lax.shift_left(high, 16) | low)
            logs += [(level * LEVEL_UNIT).astype(jnp.int32), size.astype(jnp.int32)]
        return jnp.concatenate(words + logs, axis=0)

    def merged(sources, r, more=None):
        levels = [x[64 + 2 * r:65 + 2 * r].astype(jnp.float32) * (1.0 / LEVEL_UNIT) for x in sources]
        sizes = [x[65 + 2 * r:66 + 2 * r].astype(jnp.float32) * (1.0 / SIZE_UNIT) for x in sources]
        peak = functools.reduce(jnp.maximum, levels + ([more[2]] if more else []))
        weights = [jnp.where(x > NONE + 20.0, jnp.exp(x - peak), 0.0) for x in levels]
        total = sum(weights)
        factors = [w * jnp.exp(size) * (1.0 / CODES) for w, size in zip(weights, sizes)]
        shift = sum(factors) * 32768.0
        upper, lower = -shift, -shift
        if more:
            weight = jnp.exp(more[2] - peak)
            total = total + weight
            upper, lower = weight * more[0] - shift, weight * more[1] - shift
        for factor, x in zip(factors, sources):
            words = x[32 * r:32 * r + 32]
            upper = upper + factor * lax.shift_right_logical(words, 16).astype(jnp.float32)
            lower = lower + factor * (words & 65535).astype(jnp.float32)
        total = jnp.maximum(total, 1e-30)
        inverse = 1.0 / total
        return upper * inverse, lower * inverse, jnp.maximum(peak + jnp.log(total), NONE)

    def softmax(n):
        dz, dy = offsets(n)
        owner_at = behind(n)
        a, b = tab[0, owner_at * 2] & 31, tab[0, owner_at * 2 + 1] & 31
        first_a, second_a, first_b, second_b = tab[1, a], tab[2, a], tab[1, b], tab[2, b]
        codes = (
            jnp.where(first_a > 0, first_a, first_b),
            jnp.where(second_a > 0, second_a, jnp.where(first_a > 0, first_b, second_b)),
        )
        rows = (jnp.where(first_a > 0, 0, 1), jnp.where(second_a > 0, 0, 1))
        found = []
        for code, row in zip(codes, rows):
            q = jnp.where(row == 1, q_all[n, 1], q_all[n, 0])
            found.append((row, *page_part(code & 15, lax.shift_right_logical(code, 4), q)))
        values = []
        for r in range(2):
            tops = [jnp.where(row == r, top, LOW) for row, top, _, _ in found]
            peak = jnp.maximum(tops[0], tops[1])
            factors = [jnp.where(row == r, jnp.exp(t - peak), 0.0) for t, (row, _, _, _) in zip(tops, found)]
            total = jnp.maximum(factors[0] * found[0][2] + factors[1] * found[1][2], 1e-30)
            inverse = 1.0 / total
            value = (factors[0] * inverse) * found[0][3] + (factors[1] * inverse) * found[1][3]
            values.append((value, jnp.maximum(peak + jnp.log(total), NONE)))
        for h in range(2):
            part_send[h, dz * 4 + dy] = encode(
                [(v[32 * h:32 * h + 32], v[64 + 32 * h:96 + 32 * h], level) for v, level in values]
            )

    fetch_pool.wait()
    fill_tab.wait()

    def lightning_pair(p, carry):
        for n in (2 * p, 2 * p + 1):
            lightning(n)
        for n in (2 * p, 2 * p + 1):

            @pl.when(n > 0)
            def _(n=n):
                lin_back(n).start()

        return carry

    def pair(p, carry):
        for n in (2 * p, 2 * p + 1):
            dz, dy = offsets(n)

            @pl.when(dy > 0)
            def _(n=n):
                half(0, 0, n, at_offset(1, 0)).wait_recv()

            @pl.when(dz > 0)
            def _(n=n):
                half(1, 0, n, at_offset(1, 0)).wait_recv()

        for n in (2 * p, 2 * p + 1):
            softmax(n)
        for n in (2 * p, 2 * p + 1):
            dz, dy = offsets(n)

            @pl.when(dz > 0)
            def _(dz=dz, dy=dy):
                part(0, dz, dy).start()

            @pl.when(dy > 0)
            def _(dz=dz, dy=dy):
                part(1, dz, dy).start()

        return carry

    lax.fori_loop(0, 8, pair, 0)
    own_last.wait()
    for copy in lasts:
        copy.wait_recv()
    fetch_state.wait()
    lax.fori_loop(0, 8, lightning_pair, 0)

    def middle(k, carry):
        d = jnp.where(k < 3, 1 + 2 * k - 3 * (k // 2), 0)
        for h in range(2):
            for e in range(1, 4):
                part(h, e if h == 0 else d, d if h == 0 else e).wait_recv()
            sources = [part_send[h, d if h == 0 else d * 4]]
            sources += [part_in[h, e * 4 + d if h == 0 else d * 4 + e] for e in range(1, 4)]
            mid_send[h, d] = encode([merged(sources, r) for r in range(2)])

            @pl.when(d > 0)
            def _(h=h):
                last(h, d).start()

        return carry

    lax.fori_loop(0, 4, middle, 0)

    def place(n, carry):
        lin_back(n).wait_recv()
        dz, dy = offsets(n)
        rows = pl.ds(pl.multiple_of(at_offset(dz, dy) * 8, 8), 8)
        for r in range(2):
            lin_out[r, rows] = lin_in[n, r]
        return carry

    for r in range(2):
        lin_out[r, pl.ds(pl.multiple_of(me * 8, 8), 8)] = lin_send[0, r]
    lax.fori_loop(1, N, place, 0)
    for r in range(2):
        y = lin_fresh[2] * lin_out[r] + lin_fresh[r]
        lin_ref[r] = y / jnp.sqrt(jnp.mean(y * y, axis=1, keepdims=True) + 1e-5)

    def finish(n, carry):
        half(0, 0, n, at_offset(1, 0)).wait_send()
        half(1, 0, n, at_offset(1, 0)).wait_send()
        lin_back(n).wait_send()
        dz, dy = offsets(n)

        @pl.when(dz > 0)
        def _():
            part(0, dz, dy).wait_send()

        @pl.when(dy > 0)
        def _():
            part(1, dz, dy).wait_send()

        return carry

    lax.fori_loop(1, N, finish, 0)
    for copy in mids + lasts:
        copy.wait_send()

    own = []
    for r in range(2):
        value, level = fresh[r], fresh_log[r:r + 1]
        own.append(
            [
                merged([mid_send[h, 0]], r, (value[32 * h:32 * h + 32], value[64 + 32 * h:96 + 32 * h], level))
                for h in range(2)
            ]
        )
    for h in range(2):
        for d in DIST:
            last(h, d).wait_recv()
    for r in range(2):
        pieces = []
        for h in range(2):
            pieces.append(merged([mid_in[h, d] for d in DIST], r, own[r][h]))
        soft_ref[r] = jnp.concatenate([pieces[0][0], pieces[1][0], pieces[0][1], pieces[1][1]], axis=0).T
    for copy in [last(h, d) for h in range(2) for d in DIST]:
        copy.wait_send()


def copy_kernel(a_ref, b_ref, c_ref, d_ref):
    c_ref[...] = a_ref[...]
    d_ref[...] = b_ref[...]


def rows_first(x):
    return x.reshape(2, 2, 64, WIDTH).transpose(0, 2, 1, 3).reshape(2, WIDTH, WIDTH)


def pairs_first(x):
    return x.reshape(2, 2, 2, 64, WIDTH).transpose(0, 1, 3, 2, 4).reshape(2, 2, WIDTH, WIDTH)


def rows_last(x):
    return x.reshape(2, 64, 2, WIDTH).transpose(0, 2, 1, 3).reshape(2, 2, 64 * WIDTH)


def shards(
    request_owner, page_list, context_len, lin_state, decay_rate, lin_query, lin_keyval, soft_query, new_keyval,
    page_pool,
):
    vmem = pl.BlockSpec(memory_space=pltpu.VMEM)
    hbm = pl.BlockSpec(memory_space=pl.ANY)
    out = [jax.ShapeDtypeStruct((2, WIDTH, WIDTH), jnp.float32)] * 2
    lin, soft = pl.pallas_call(
        kernel,
        out_shape=[pltpu.VMEM((2, WIDTH, WIDTH), jnp.float32)] * 2,
        in_specs=[hbm] * 10,
        out_specs=[vmem] * 2,
        scratch_shapes=[
            pltpu.VMEM(lin_state.shape, jnp.float32),
            pltpu.VMEM(page_pool.shape, jnp.bfloat16),
            pltpu.VMEM((1, 32), jnp.int32),
            pltpu.VMEM((8, 32), jnp.int32),
            pltpu.VMEM((1, 32), jnp.int32),
            pltpu.VMEM((1, 64), jnp.float32),
            pltpu.VMEM((2, WIDTH, WIDTH), jnp.bfloat16),
            pltpu.VMEM(new_keyval.shape, jnp.bfloat16),
            pltpu.VMEM((2, WIDTH, WIDTH), jnp.bfloat16),
            pltpu.VMEM((2, 2, WIDTH, WIDTH), jnp.bfloat16),
            pltpu.VMEM((3, WIDTH, WIDTH), jnp.float32),
            pltpu.VMEM((2, WIDTH, WIDTH), jnp.float32),
            pltpu.VMEM((2, WIDTH, WIDTH), jnp.float32),
            pltpu.VMEM((8, WIDTH), jnp.float32),
            pltpu.VMEM((N, 2, WIDTH, WIDTH), jnp.bfloat16),
            pltpu.VMEM((4, 4, 16, WIDTH), jnp.bfloat16),
            pltpu.VMEM((4, 4, 16, WIDTH), jnp.bfloat16),
            pltpu.VMEM((4, 4, 16, WIDTH), jnp.bfloat16),
            pltpu.VMEM((N, 2, 8, WIDTH), jnp.float32),
            pltpu.VMEM((N, 2, 8, WIDTH), jnp.float32),
            pltpu.VMEM((2, N, 68, WIDTH), jnp.int32),
            pltpu.VMEM((2, N, 68, WIDTH), jnp.int32),
            pltpu.VMEM((2, 4, 68, WIDTH), jnp.int32),
            pltpu.VMEM((2, 4, 68, WIDTH), jnp.int32),
            pltpu.VMEM((8, WIDTH), jnp.int32),
            pltpu.SMEM((8, WIDTH), jnp.int32),
            pltpu.SemaphoreType.DMA((13,)),
            pltpu.SemaphoreType.DMA((2, N)),
            pltpu.SemaphoreType.DMA((2, N)),
            pltpu.SemaphoreType.DMA((2, 4)),
            pltpu.SemaphoreType.DMA((2, 4)),
            pltpu.SemaphoreType.DMA((N,)),
            pltpu.SemaphoreType.DMA((N,)),
            pltpu.SemaphoreType.DMA((2, N)),
            pltpu.SemaphoreType.DMA((2, N)),
            pltpu.SemaphoreType.DMA((2, 4)),
            pltpu.SemaphoreType.DMA((2, 4)),
        ],
        compiler_params=pltpu.CompilerParams(
            collective_id=0, has_side_effects=True, vmem_limit_bytes=56 * 1024 * 1024
        ),
    )(
        request_owner.reshape(1, 32), page_list.T, context_len.reshape(1, 32), decay_rate.reshape(1, 64),
        rows_first(soft_query), new_keyval, rows_first(lin_query), pairs_first(lin_keyval), lin_state, page_pool,
    )
    lin, soft = (pltpu.with_memory_space_constraint(x, pltpu.VMEM) for x in (lin, soft))
    lin, soft = pl.pallas_call(copy_kernel, out_shape=out, in_specs=[vmem] * 2, out_specs=[vmem] * 2)(lin, soft)
    return rows_last(lin), rows_last(soft)


def solution(mesh):
    return jax.shard_map(
        shards,
        mesh=mesh,
        in_specs=(
            P("grp"), P("grp", None), P("grp"), P("grp", "head", None, None), P(),
            P(("grp", "head"), None, None), P(("grp", "head"), None, None, None),
            P(("grp", "head"), None, None), P(("grp", "head"), None, None, None),
            P(("grp", "head"), None, None, None),
        ),
        out_specs=(P(("grp", "head"), None, None), P(("grp", "head"), None, None)),
        check_vma=False,
    )
```
